128 devices in a mesh: dp: 16 (over y, x_hi, core), tensor: 8 (over x_lo, z).
Axes of the slice: x: 4 (x_hi: 2, x_lo: 2; x = x_hi * 2 + x_lo), y: 4, z: 4, core: 2. Of those that a mesh axis runs over, the one named last changes fastest.
Arguments:
- token_ids: int32 [1024, 4], P('dp'), may hold values from 0 to 76799
- lengths: int32 [1024], P('dp'), may hold values from 1 to 512, as said below
- embed_table: bfloat16 [76800, 5120], P('dp', 'tensor'), may hold values from -6 to 6
- norm_gain: bfloat16 [5120], P('tensor'), may hold values from 0.099609375 to 1.8984375
- w_query: bfloat16 [5120, 8192], P(('dp', 'tensor')), may hold values from -0.078125 to 0.078125
- w_key: bfloat16 [5120, 1024], P(('dp', 'tensor')), may hold values from -0.078125 to 0.078125
- w_value: bfloat16 [5120, 1024], P(('dp', 'tensor')), may hold values from -0.078125 to 0.078125
- w_out: bfloat16 [8192, 5120], P(('dp', 'tensor')), may hold values from -0.0625 to 0.0625
- q_gain: bfloat16 [128], replicated, may hold values from 0.099609375 to 1.8984375
- k_gain: bfloat16 [128], replicated, may hold values from 0.099609375 to 1.8984375
- key_cache: bfloat16 [1024, 512, 1024], P('dp', None, 'tensor'), may hold values from -160 to 160
- value_cache: bfloat16 [1024, 512, 1024], P('dp', None, 'tensor'), may hold values from -6 to 6
Outputs:
- attended: bfloat16 [1024, 4, 5120], P('dp', None, 'tensor')
- new_keys: bfloat16 [1024, 4, 1024], P('dp', None, 'tensor')
- new_values: bfloat16 [1024, 4, 1024], P('dp', None, 'tensor')
The draws below stay inside these ranges and needn't reach their ends.
Inputs may be any that keep to these rules, and one draw needn't show every extreme that they name: `lengths`: at least one row holds 512 cached positions.
All inputs are finite; a program needn't handle non-finite values.
Results may differ from the reference program's by a relative error of at most 0.0066.
Values may be sent and summed in bfloat16 or wider, within the bound.
A program may use at most 192 MiB of HBM per device.

```python
import math
import jax
import jax.numpy as jnp
import numpy as np
from jax import lax

D = 5120
HQ = 64
KVH = 8
HD = 128
V = 76800
CACHE = 512
STEPS = 4
ROWS = 1024
QW = 8192
KW = 1024


def draw_lengths(key, part):
    key = jax.random.fold_in(key, 11)
    first, second = jax.random.split(key)
    drawn = jax.random.randint(first, (ROWS,), 1, CACHE + 1)
    spot = jax.random.randint(second, (), 0, ROWS)
    return jnp.where(jnp.arange(ROWS) == spot, CACHE, drawn).astype(jnp.int32)


def draw_key_cache(key, part):
    key = jax.random.fold_in(key, 12)
    first = jax.random.fold_in(key, 0)
    base = jnp.clip(jax.random.normal(first, (ROWS, CACHE, KW), jnp.float32), -6.0, 6.0)
    return base.astype(jnp.bfloat16)


def place_ends(values, key, least, high):
    index_at = [jax.random.randint(jax.random.fold_in(key, axis), (), 0, length) for axis, length in enumerate(values.shape)]
    main_axis = values.shape.index(max(values.shape))
    next_to = index_at[:main_axis] + [(index_at[main_axis] + 1) % values.shape[main_axis]] + index_at[main_axis + 1:]
    return values.at[tuple(index_at)].set(least).at[tuple(next_to)].set(high)


def level_of(stream_key, extent, cuts, least, largest):
    def one(position, blocks):
        steps = jax.random.uniform(jax.random.fold_in(jax.random.fold_in(stream_key, 6), position), (blocks,), jnp.float32, least / len(cuts), largest / len(cuts))
        return jnp.repeat(jnp.exp(steps), extent[position] // blocks).reshape((-1,) + (1,) * (len(extent) - position - 1))

    level = one(*cuts[0])
    for cut in cuts[1:]:
        level = level * one(*cut)
    return level


def wide_ids(rng, shape, count, slope):
    weights = [min(1 << octave, count + 1 - (1 << octave)) * (1 << 20) // math.isqrt((1 << octave) ** slope) + 1 for octave in range((count + 1).bit_length()) if 1 << octave <= count]
    deviation = 1 + sum(weights) // (1 << 30)
    listing = np.cumsum(np.array([max(1, weight // deviation) for weight in weights]))
    ticket = jax.random.randint(jax.random.fold_in(rng, 1), shape, 0, int(listing[len(weights) - 1]))
    start = jnp.left_shift(1, jnp.searchsorted(jnp.asarray(listing, jnp.int32), ticket, side="right").astype(jnp.int32))
    grade = start - 1 + jax.random.randint(jax.random.fold_in(rng, 4), shape, 0, 1 << 30) % jnp.minimum(start, count + 1 - start)
    return jax.random.permutation(jax.random.fold_in(rng, 2), count)[grade].astype(jnp.int32)


def scatter_about(stream_key, extent, deviation, limit, cuts=(), kind=jnp.bfloat16):
    factor_of = level_of(stream_key, extent, cuts, -0.22, 0.18) if cuts else 1.0
    entries = jax.random.normal(stream_key, extent, jnp.float32) * deviation * factor_of
    return jnp.minimum(jnp.maximum(entries, -limit), limit).astype(kind)


def setup_inputs(seed: int = 0) -> dict:
    splits = jax.random.split(jax.random.key(seed), 13)
    token_ids = place_ends(wide_ids(splits[0], (ROWS, STEPS), V, 2), jax.random.fold_in(splits[0], 3), 0, V - 1).astype(jnp.int32)
    lengths = draw_lengths(jax.random.fold_in(splits[12], 71), 0)
    embed_table = scatter_about(splits[2], (V, D), 1.0, 6.0, ((0, 16), (1, 8)))
    norm_gain = jnp.clip(1.0 + 0.18 * jax.random.normal(splits[3], (D,), jnp.float32), 0.099609375, 1.8984375).astype(jnp.bfloat16)
    w_query = scatter_about(splits[4], (D, QW), D ** -0.5, 0.078125, ((0, 128),))
    w_key = scatter_about(splits[5], (D, KW), D ** -0.5, 0.078125, ((0, 128),))
    w_value = scatter_about(splits[6], (D, KW), D ** -0.5, 0.078125, ((0, 128),))
    w_out = scatter_about(splits[7], (QW, D), QW ** -0.5, 0.0625, ((0, 128),))
    q_gain = jnp.clip(1.0 + 0.18 * jax.random.normal(splits[8], (HD,), jnp.float32), 0.099609375, 1.8984375).astype(jnp.bfloat16)
    k_gain = jnp.clip(1.0 + 0.18 * jax.random.normal(splits[9], (HD,), jnp.float32), 0.099609375, 1.8984375).astype(jnp.bfloat16)
    key_cache = draw_key_cache(jax.random.fold_in(splits[12], 71), 0)
    value_cache = scatter_about(splits[11], (ROWS, CACHE, KW), 1.0, 6.0, ((0, 16), (2, 8)))
    return {"token_ids": token_ids, "lengths": lengths, "embed_table": embed_table, "norm_gain": norm_gain, "w_query": w_query, "w_key": w_key, "w_value": w_value, "w_out": w_out, "q_gain": q_gain, "k_gain": k_gain, "key_cache": key_cache, "value_cache": value_cache}


EPS = 1e-06
THETA = 1000000.0

def rms_scale(values, gain):
    mean_sq = lax.optimization_barrier(jnp.mean(values * values, axis=-1, keepdims=True))
    return values * lax.rsqrt(mean_sq + EPS) * gain.astype(jnp.float32)

def rotate(values, positions):
    half = values.shape[-1] // 2
    freq = THETA ** (-jnp.arange(half, dtype=jnp.float32) * 2.0 / values.shape[-1])
    angle = positions.astype(jnp.float32)[:, :, None, None] * freq
    cosine = jnp.cos(angle)
    sine = jnp.sin(angle)
    first = values[..., :half]
    second = values[..., half:]
    return jnp.concatenate([first * cosine - second * sine, second * cosine + first * sine], axis=-1)

def attend(query, fresh_keys, fresh_values, key_cache, value_cache, lengths):
    rows, steps, heads_count, width = query.shape
    kv_heads = fresh_keys.shape[2]
    group = heads_count // kv_heads
    cache_len = key_cache.shape[1]
    grouped = query.astype(jnp.float32).reshape(rows, steps, kv_heads, group, width)
    keys = key_cache.astype(jnp.float32).reshape(rows, cache_len, kv_heads, width)
    values = value_cache.astype(jnp.float32).reshape(rows, cache_len, kv_heads, width)
    scale = 1.0 / math.sqrt(width)
    old_scores = jnp.einsum('rskgd,rckd->rkgsc', grouped, keys) * scale
    new_scores = jnp.einsum('rskgd,rtkd->rkgst', grouped, fresh_keys.astype(jnp.float32)) * scale
    valid = jnp.arange(cache_len)[None, :] < lengths[:, None]
    old_scores = jnp.where(valid[:, None, None, None, :], old_scores, -jnp.inf)
    causal = jnp.arange(steps)[None, :] <= jnp.arange(steps)[:, None]
    new_scores = jnp.where(causal[None, None, None, :, :], new_scores, -jnp.inf)
    highest = jnp.maximum(lax.optimization_barrier(jnp.max(old_scores, axis=-1)), lax.optimization_barrier(jnp.max(new_scores, axis=-1)))
    old_exp = jnp.exp(old_scores - highest[..., None])
    new_exp = jnp.exp(new_scores - highest[..., None])
    total = lax.optimization_barrier(jnp.sum(old_exp, axis=-1)) + lax.optimization_barrier(jnp.sum(new_exp, axis=-1))
    old_weights = (old_exp / total[..., None]).astype(jnp.bfloat16).astype(jnp.float32)
    new_weights = (new_exp / total[..., None]).astype(jnp.bfloat16).astype(jnp.float32)
    mixed = jnp.einsum('rkgsc,rckd->rskgd', old_weights, values)
    mixed = mixed + jnp.einsum('rkgst,rtkd->rskgd', new_weights, fresh_values.astype(jnp.float32))
    return mixed.reshape(rows, steps, heads_count * width).astype(jnp.bfloat16)

def reference(token_ids, lengths, embed_table, norm_gain, w_query, w_key, w_value, w_out, q_gain, k_gain, key_cache, value_cache):
    embedded = jnp.take(embed_table, token_ids, axis=0)
    wide = embedded.astype(jnp.float32)
    normed = rms_scale(wide, norm_gain).astype(jnp.bfloat16)
    flat = normed.reshape(ROWS * STEPS, D)
    query_raw = jnp.dot(flat, w_query, preferred_element_type=jnp.float32).reshape(ROWS, STEPS, HQ, HD)
    key_raw = jnp.dot(flat, w_key, preferred_element_type=jnp.float32).reshape(ROWS, STEPS, KVH, HD)
    fresh_values = jnp.dot(flat, w_value, preferred_element_type=jnp.float32).astype(jnp.bfloat16)
    fresh_values = fresh_values.reshape(ROWS, STEPS, KVH, HD)
    positions = lengths[:, None] + jnp.arange(STEPS, dtype=jnp.int32)[None, :]
    query = rotate(rms_scale(query_raw, q_gain), positions).astype(jnp.bfloat16)
    fresh_keys = rotate(rms_scale(key_raw, k_gain), positions).astype(jnp.bfloat16)
    block = math.gcd(ROWS, 64)
    count = ROWS // block

    def one_block(pieces):
        return attend(*pieces)
    heads = lax.map(one_block, (query.reshape(count, block, STEPS, HQ, HD), fresh_keys.reshape(count, block, STEPS, KVH, HD), fresh_values.reshape(count, block, STEPS, KVH, HD), key_cache.reshape(count, block, CACHE, KW), value_cache.reshape(count, block, CACHE, KW), lengths.reshape(count, block)))
    heads = heads.reshape(ROWS * STEPS, QW)
    output = jnp.dot(heads, w_out, preferred_element_type=jnp.float32) + wide.reshape(ROWS * STEPS, D)
    attended = output.astype(jnp.bfloat16).reshape(ROWS, STEPS, D)
    return (attended, fresh_keys.reshape(ROWS, STEPS, KW), fresh_values.reshape(ROWS, STEPS, KW))
```

```python
import math

import jax
import jax.numpy as jnp
from jax import lax
from jax.experimental import pallas as pl
from jax.experimental.pallas import tpu as pltpu
from jax.sharding import PartitionSpec as P

EPS = 1e-06
THETA = 1000000.0
SLOTS = 64
LANES = 128
EXTRA = 16
MESH = pl.DeviceIdType.MESH
NT = (((1,), (1,)), ((), ()))


class Place:
    def __init__(self):
        self.dp = lax.axis_index("dp")
        self.t = lax.axis_index("tensor")
        self.y, self.xh, self.c = self.dp // 4, (self.dp // 2) % 2, self.dp % 2
        self.xl, self.z = self.t // 4, self.t % 4

    def dp_id(self, dy, dxh, dc=0):
        return ((self.y + dy) % 4) * 4 + ((self.xh + dxh) % 2) * 2 + (self.c + dc) % 2

    def t_id(self, dxl, dz):
        return ((self.xl + dxl) % 2) * 4 + (self.z + dz) % 4


def remote(src, dst, sems, k, device):
    return pltpu.make_async_remote_copy(
        src_ref=src,
        dst_ref=dst,
        send_sem=sems.at[0, k],
        recv_sem=sems.at[1, k],
        device_id=device,
        device_id_type=MESH,
    )


def greet(devices):
    barrier = pltpu.get_barrier_semaphore()
    for device in devices:
        pl.semaphore_signal(barrier, inc=1, device_id=device, device_id_type=MESH)
    pl.semaphore_wait(barrier, len(devices))


class PairRing:
    COPIES = 9

    def __init__(self, own, block, first, second, ident, device, sems, landed=None):
        self.landed = landed or (lambda k, e: None)
        self.ident = ident
        pair, nxt, prv = device(0, 1), device(1, 0), device(3, 0)
        me, mate = ident(0, 0), ident(0, 1)
        self.c = [
            remote(own, block(me), sems, 0, pair),
            remote(own, block(me), sems, 1, nxt),
            remote(own, block(me), sems, 2, prv),
            remote(block(mate), block(mate), sems, 3, nxt),
            remote(block(mate), block(mate), sems, 4, prv),
            remote(first(ident(3, 0)), first(ident(3, 0)), sems, 5, nxt),
            remote(second(ident(1, 0)), second(ident(1, 0)), sems, 6, prv),
            remote(first(ident(3, 1)), first(ident(3, 1)), sems, 7, nxt),
            remote(second(ident(1, 1)), second(ident(1, 1)), sems, 8, prv),
        ]

    def s0(self):
        self.c[0].start()
        self.c[1].start()
        self.c[2].start()

    def s1(self):
        self.c[0].wait_recv()
        self.c[3].start()
        self.c[4].start()
        self.landed(0, 1)

    def s2(self):
        self.c[1].wait_recv()
        self.c[5].start()
        self.landed(3, 0)
        self.c[2].wait_recv()
        self.c[6].start()
        self.landed(1, 0)

    def s3(self):
        self.c[3].wait_recv()
        self.c[7].start()
        self.landed(3, 1)
        self.c[4].wait_recv()
        self.c[8].start()
        self.landed(1, 1)

    def s4(self):
        self.c[5].wait_recv()
        self.c[6].wait_recv()
        self.landed(2, 0)
        self.c[7].wait_recv()
        self.c[8].wait_recv()
        self.landed(2, 1)

    def end(self):
        for copy in self.c:
            copy.wait_send()


class CoreShare:
    COPIES = 8

    def __init__(self, block, place, sems):
        self.block, self.place, self.sems = block, place, sems
        self.started = []

    def give(self, src, k, e):
        p = self.place
        copy = remote(
            src, self.block(p.dp_id(k, e)), self.sems, k * 2 + e, (p.dp_id(0, 0, 1), p.t)
        )
        copy.start()
        self.started.append(copy)

    def end(self):
        for copy in self.started:
            copy.wait()


def fetch_kernel(
    req, slot, gain, table, wq, wk, wv, wo,
    w_all, wo_part, e_all, flag,
    reqs, table_v, index_v, slots_out, slots_in, e_own,
    req_sems, slot_sems, p1_sems, o1_sems, ring_sems, core_sems, e_sems, local_sems,
):
    p = Place()
    dp, t = p.dp, p.t
    owners, tensors = reqs.shape[0], e_all.shape[0]
    vocab = table.shape[0]
    qw, kw = wq.shape[1] // tensors, wk.shape[1] // tensors
    ow = wo.shape[1] // tensors
    dp_peers = [(lax.rem(dp + j, owners), t) for j in range(1, owners)]
    t_peers = [(dp, lax.rem(t + j, tensors)) for j in range(1, tensors)]
    greet(dp_peers + t_peers)

    asks = []
    for j in range(1, owners):
        to = lax.rem(dp + j, owners)
        copy = remote(req.at[to], reqs.at[dp], req_sems, j, (to, t))
        copy.start()
        asks.append(copy)
    own_ask = pltpu.make_async_copy(req.at[dp], reqs.at[dp], local_sems.at[0])
    own_ask.start()
    load_table = pltpu.make_async_copy(table, table_v.at[pl.ds(0, vocab)], local_sems.at[1])
    load_table.start()

    row = dp * tensors + t
    parts = ((wq, qw, 0), (wk, kw, qw), (wv, kw, qw + kw))
    first = []
    for j in range(1, tensors):
        to = lax.rem(t + j, tensors)
        for a, (w, n, at) in enumerate(parts):
            copy = remote(
                w.at[:, pl.ds(pl.multiple_of(to * n, LANES), n)],
                w_all.at[row, :, pl.ds(at, n)],
                p1_sems, j * 3 + a, (dp, to),
            )
            copy.start()
            first.append(copy)
    stays = []
    for a, (w, n, at) in enumerate(parts):
        copy = pltpu.make_async_copy(
            w.at[:, pl.ds(pl.multiple_of(t * n, LANES), n)],
            w_all.at[row, :, pl.ds(at, n)],
            local_sems.at[2 + a],
        )
        copy.start()
        stays.append(copy)
    copy = pltpu.make_async_copy(
        wo.at[:, pl.ds(pl.multiple_of(t * ow, LANES), ow)], wo_part.at[t], local_sems.at[5]
    )
    copy.start()
    stays.append(copy)

    pad = table_v.shape[0] - vocab
    table_v[pl.ds(vocab, pad), :] = jnp.zeros((pad, table_v.shape[1]), table_v.dtype)
    for copy in asks:
        copy.wait_recv()
    own_ask.wait()
    asked = jnp.concatenate(
        [reqs[lax.rem(dp + j, owners), 0:1, :] for j in range(owners)], axis=0
    )
    over = jnp.max(jnp.where(lax.broadcasted_iota(jnp.int32, asked.shape, 1) == SLOTS, asked, 0))
    flag[...] = jnp.full(flag.shape, over, jnp.int32)
    columns = jnp.transpose(asked)
    for j in range(owners):
        index_v[j * SLOTS:(j + 1) * SLOTS, :] = jnp.broadcast_to(
            columns[:SLOTS, j:j + 1], (SLOTS, LANES)
        )
    load_table.wait()
    chunk = 4
    replies = []
    for m in range(owners // chunk):
        wanted = index_v[m * chunk * SLOTS:(m + 1) * chunk * SLOTS, 0:1]
        place = lax.broadcasted_iota(jnp.int32, (chunk * SLOTS, table_v.shape[0]), 1)
        hit = (place == wanted).astype(jnp.float32).astype(jnp.bfloat16)
        rows = jnp.dot(hit, table_v[...], preferred_element_type=jnp.float32)
        slots_out[m * chunk:(m + 1) * chunk] = rows.astype(jnp.bfloat16).reshape(
            chunk, SLOTS, rows.shape[1]
        )
        for j in range(m * chunk, (m + 1) * chunk):
            if j == 0:
                copy = pltpu.make_async_copy(slots_out.at[0], slots_in.at[dp], local_sems.at[6])
            else:
                copy = remote(
                    slots_out.at[j], slots_in.at[dp], slot_sems, j, (lax.rem(dp + j, owners), t)
                )
            copy.start()
            replies.append(copy)

    for copy in first:
        copy.wait_recv()
    for copy in stays:
        copy.wait()

    def block(i):
        return w_all.at[pl.ds(i * tensors, tensors)]

    half = tensors // 2
    share = CoreShare(block, p, core_sems)
    ring = PairRing(
        block(dp),
        block,
        lambda i: w_all.at[pl.ds(i * tensors, half)],
        lambda i: w_all.at[pl.ds(i * tensors + half, half)],
        lambda k, e: p.dp_id(k, e),
        lambda k, e: (p.dp_id(k, e), t),
        ring_sems,
        lambda k, e: share.give(block(p.dp_id(k, e)), k, e),
    )
    ring.s0()
    share.give(block(dp), 0, 0)

    replies[0].wait()
    for copy in replies[1:]:
        copy.wait_recv()
    picks = lax.broadcasted_iota(jnp.int32, (slot.shape[0], owners * SLOTS), 1) == slot[...]
    tokens = slot.shape[0]
    e_own[0:tokens] = jnp.dot(
        picks.astype(jnp.float32).astype(jnp.bfloat16),
        slots_in[...].reshape(owners * SLOTS, slots_in.shape[2]),
        preferred_element_type=jnp.float32,
    ).astype(jnp.bfloat16)
    e_own[tokens:] = jnp.broadcast_to(gain[...], (EXTRA, gain.shape[1]))
    e_ring = PairRing(
        e_own,
        lambda i: e_all.at[i],
        lambda i: e_all.at[i, pl.ds(0, tokens // 2)],
        lambda i: e_all.at[i, pl.ds(tokens // 2, tokens // 2 + EXTRA)],
        lambda k, e: p.t_id(e, k),
        lambda k, e: (dp, p.t_id(e, k)),
        e_sems,
    )
    e_ring.s0()
    keep = pltpu.make_async_copy(e_own, e_all.at[t], local_sems.at[7])
    keep.start()
    ring.s1()
    e_ring.s1()
    e_ring.s2()
    ring.s2()
    e_ring.s3()
    outs = []
    for j in range(1, tensors):
        to = lax.rem(t + j, tensors)
        copy = remote(
            wo.at[:, pl.ds(pl.multiple_of(to * ow, LANES), ow)],
            wo_part.at[t],
            o1_sems, j, (dp, to),
        )
        copy.start()
        outs.append(copy)
    ring.s3()
    e_ring.s4()
    ring.s4()
    for copy in outs:
        copy.wait()
    for copy in first + asks + replies[1:]:
        copy.wait_send()
    keep.wait()
    ring.end()
    e_ring.end()
    share.end()


def fetch(req, slot, gain, table, wq, wk, wv, wo):
    owners, tensors = lax.axis_size("dp"), lax.axis_size("tensor")
    tokens = slot.shape[0]
    features = table.shape[1]
    height, depth = wq.shape[0], wo.shape[0]
    wide = (wq.shape[1] + wk.shape[1] + wv.shape[1]) // tensors
    padded = -(-table.shape[0] // LANES) * LANES
    anywhere, vmem = pl.BlockSpec(memory_space=pl.ANY), pl.BlockSpec(memory_space=pltpu.VMEM)
    dma = pltpu.SemaphoreType.DMA
    bf16 = jnp.bfloat16
    return pl.pallas_call(
        fetch_kernel,
        out_shape=(
            jax.ShapeDtypeStruct((owners * tensors, height, wide), bf16),
            jax.ShapeDtypeStruct((tensors, depth, wo.shape[1] // tensors), bf16),
            jax.ShapeDtypeStruct((tensors, tokens + EXTRA, features), bf16),
            jax.ShapeDtypeStruct((8, LANES), jnp.int32),
        ),
        in_specs=[anywhere, vmem, vmem] + [anywhere] * 5,
        out_specs=(anywhere, anywhere, anywhere, vmem),
        scratch_shapes=[
            pltpu.VMEM((owners, 8, LANES), jnp.int32),
            pltpu.VMEM((padded, features), bf16),
            pltpu.VMEM((owners * SLOTS, LANES), jnp.int32),
            pltpu.VMEM((owners, SLOTS, features), bf16),
            pltpu.VMEM((owners, SLOTS, features), bf16),
            pltpu.VMEM((tokens + EXTRA, features), bf16),
            dma((2, owners)),
            dma((2, owners)),
            dma((2, 3 * tensors)),
            dma((2, tensors)),
            dma((2, PairRing.COPIES)),
            dma((2, CoreShare.COPIES)),
            dma((2, PairRing.COPIES)),
            dma((8,)),
        ],
        compiler_params=pltpu.CompilerParams(
            collective_id=1, has_side_effects=True, vmem_limit_bytes=40 * 1024 * 1024
        ),
        name="fetch",
    )(req, slot, gain, table, wq, wk, wv, wo)


ROWS_AT_ONCE = 4
PIECES = 4


def block_kernel(
    lengths, e_all, w_all, wo_part, q_gain, k_gain, cosine, sine, key_cache, value_cache,
    attended, new_keys, new_values,
    e_v, w_v, wo_v, heads_v, acc_v, nk_v, nv_v, k_v, v_v, total_v,
    w_sems, kv_sems, ring_sems, core_sems, heads_sems, local_sems,
):
    p = Place()
    dp, t = p.dp, p.t
    tensors, features = e_v.shape[0], e_v.shape[2]
    tokens = attended.shape[0]
    width = LANES
    rows, cache = key_cache.shape[0], key_cache.shape[1]
    steps = tokens // rows
    qw = heads_v.shape[2]
    heads = qw // width
    greet(
        [(p.dp_id(0, 0, 1), t), (p.dp_id(0, 1), t), (p.dp_id(1, 0), t), (p.dp_id(3, 0), t)]
        + [(dp, p.t_id(1, 0)), (dp, p.t_id(0, 1)), (dp, p.t_id(0, 3))]
    )

    load_e = pltpu.make_async_copy(e_all, e_v, local_sems.at[0])
    load_e.start()
    loads = [pltpu.make_async_copy(w_all.at[i], w_v.at[i], w_sems.at[i]) for i in range(tensors)]
    for copy in loads:
        copy.start()

    def block(i):
        return wo_v.at[pl.ds(i * tensors, tensors)]

    half = tensors // 2
    share = CoreShare(block, p, core_sems)
    ring = PairRing(
        wo_part,
        block,
        lambda i: wo_v.at[pl.ds(i * tensors, half)],
        lambda i: wo_v.at[pl.ds(i * tensors + half, half)],
        lambda k, e: p.dp_id(k, e),
        lambda k, e: (p.dp_id(k, e), t),
        ring_sems,
        lambda k, e: share.give(block(p.dp_id(k, e)), k, e),
    )
    ring.s0()
    share.give(wo_part, 0, 0)
    keep = pltpu.make_async_copy(wo_part, block(dp), local_sems.at[1])
    keep.start()

    piece = rows // PIECES

    def load_kv(i):
        at = pl.ds(i * piece, piece)
        return (
            pltpu.make_async_copy(key_cache.at[at], k_v.at[i % 2], kv_sems.at[0, i]),
            pltpu.make_async_copy(value_cache.at[at], v_v.at[i % 2], kv_sems.at[1, i]),
        )

    caches = [load_kv(i) for i in range(PIECES)]
    for copy in caches[0] + caches[1]:
        copy.start()

    load_e.wait()

    def square(i, total):
        wide = e_v[i, pl.ds(0, tokens)].astype(jnp.float32)
        return total + jnp.sum(wide * wide, axis=-1, keepdims=True)

    total = lax.fori_loop(0, tensors, square, jnp.zeros((tokens, 1), jnp.float32))
    inverse = lax.rsqrt(total / (tensors * features) + EPS)
    for i in range(tensors):
        loads[i].wait()

    def project(i, carry):
        gain = e_v[i, pl.ds(tokens, EXTRA)].astype(jnp.float32)[0:1]
        normed = e_v[i, pl.ds(0, tokens)].astype(jnp.float32) * inverse * gain
        part = jnp.dot(normed.astype(jnp.bfloat16), w_v[i], preferred_element_type=jnp.float32)
        acc_v[...] = acc_v[...] + part
        return carry

    acc_v[...] = jnp.zeros(acc_v.shape, jnp.float32)
    lax.fori_loop(0, tensors, project, 0)

    def placed(raw, head_gain):
        mean_sq = jnp.mean(raw * raw, axis=-1, keepdims=True)
        scaled = raw * lax.rsqrt(mean_sq + EPS) * head_gain
        return scaled * cosine[...] + pltpu.roll(scaled, width // 2, 1) * sine[...]

    head_gain = q_gain[...].astype(jnp.float32)
    for h in range(heads):
        at = slice(h * width, (h + 1) * width)
        acc_v[:, at] = placed(acc_v[:, at], head_gain)
    nk_v[...] = placed(acc_v[:, qw:qw + width], k_gain[...].astype(jnp.float32)).astype(jnp.bfloat16)
    nv_v[...] = acc_v[:, qw + width:qw + 2 * width].astype(jnp.bfloat16)
    new_keys[...] = nk_v[...]
    new_values[...] = nv_v[...]
    ring.s1()

    scale = 1.0 / math.sqrt(width)
    pair = 2 * steps
    group = ROWS_AT_ONCE * steps
    query = lax.broadcasted_iota(jnp.int32, (heads * pair, 1), 0) % pair
    is_first = query < steps
    fresh = lax.broadcasted_iota(jnp.int32, (heads * pair, group), 1)
    column = lax.broadcasted_iota(jnp.int32, (heads * pair, cache), 1)

    def attend(i, g):
        at = pl.ds(pl.multiple_of(i * piece * steps + g * group, group), group)
        queries = acc_v[at, 0:qw]
        keys, values = nk_v[at, :], nv_v[at, :]
        results = []
        for n in range(ROWS_AT_ONCE // 2):
            q = jnp.concatenate(
                [
                    queries[n * pair:(n + 1) * pair, h * width:(h + 1) * width]
                    for h in range(heads)
                ],
                axis=0,
            ).astype(jnp.bfloat16)
            r = g * ROWS_AT_ONCE + 2 * n
            old_a = lax.dot_general(q, k_v[i % 2, r], NT, preferred_element_type=jnp.float32)
            old_b = lax.dot_general(q, k_v[i % 2, r + 1], NT, preferred_element_type=jnp.float32)
            new = lax.dot_general(q, keys, NT, preferred_element_type=jnp.float32) * scale
            token = query + n * pair
            new = jnp.where((fresh // steps == token // steps) & (fresh <= token), new, -jnp.inf)
            held = jnp.where(
                is_first, lengths[i * piece + r], lengths[i * piece + r + 1]
            )
            old = jnp.where(is_first, old_a, old_b) * scale
            old = jnp.where(column < held, old, -jnp.inf)
            top = jnp.maximum(
                jnp.max(old, axis=-1, keepdims=True), jnp.max(new, axis=-1, keepdims=True)
            )
            old = jnp.exp(old - top)
            new = jnp.exp(new - top)
            whole = jnp.sum(old, axis=-1, keepdims=True) + jnp.sum(new, axis=-1, keepdims=True)
            inv = 1.0 / whole
            old = (old * inv).astype(jnp.bfloat16)
            new = (new * inv).astype(jnp.bfloat16)
            out_a = jnp.dot(old, v_v[i % 2, r], preferred_element_type=jnp.float32)
            out_b = jnp.dot(old, v_v[i % 2, r + 1], preferred_element_type=jnp.float32)
            out = jnp.where(is_first, out_a, out_b)
            out = out + jnp.dot(new, values, preferred_element_type=jnp.float32)
            results.append(
                jnp.concatenate([out[h * pair:(h + 1) * pair] for h in range(heads)], axis=1)
            )
        heads_v[t, at, :] = jnp.concatenate(results, axis=0).astype(jnp.bfloat16)

    halves = 2
    span = tokens // halves
    rings = []
    for j in range(halves):
        rings.append(
            PairRing(
                heads_v.at[t, pl.ds(j * span, span)],
                lambda i, j=j: heads_v.at[i, pl.ds(j * span, span)],
                lambda i, j=j: heads_v.at[i, pl.ds(j * span, span // 2)],
                lambda i, j=j: heads_v.at[i, pl.ds(j * span + span // 2, span // 2)],
                lambda k, e: p.t_id(e, k),
                lambda k, e: (dp, p.t_id(e, k)),
                heads_sems.at[j],
            )
        )
    for i in range(PIECES):
        for copy in caches[i]:
            copy.wait()

        def one(g, carry):
            attend(i, g)
            return carry

        lax.fori_loop(0, piece // ROWS_AT_ONCE, one, 0)
        if i + 2 < PIECES:
            for copy in caches[i + 2]:
                copy.start()
        if i == PIECES // 2 - 1:
            rings[0].s0()
            ring.s2()
        if i == PIECES // 2:
            rings[0].s1()
    rings[1].s0()
    rings[0].s2()
    ring.s3()
    rings[1].s1()
    rings[0].s3()
    rings[1].s2()
    rings[1].s3()
    ring.s4()
    rings[0].s4()
    rings[1].s4()
    keep.wait()
    share.end()

    def back(i, carry):
        w = wo_v[pl.ds(i * (owners_per(tensors, wo_v)), owners_per(tensors, wo_v))]
        w = w.reshape(qw, w.shape[-1])
        total_v[...] = total_v[...] + jnp.dot(heads_v[i], w, preferred_element_type=jnp.float32)
        return carry

    total_v[...] = e_v[t, pl.ds(0, tokens)].astype(jnp.float32)
    lax.fori_loop(0, tensors, back, 0)
    attended[...] = total_v[...].astype(jnp.bfloat16)
    ring.end()
    rings[0].end()
    rings[1].end()


def owners_per(tensors, wo_v):
    return wo_v.shape[0] // tensors


def decode(lengths, e_all, w_all, wo_part, q_gain, k_gain, cosine, sine, keys, values):
    owners, tensors = lax.axis_size("dp"), lax.axis_size("tensor")
    held, features = e_all.shape[1:]
    tokens = held - EXTRA
    rows, cache, width = keys.shape
    wide = w_all.shape[-1]
    depth, ow = wo_part.shape[1:]
    qw = wide - 2 * width
    piece = rows // PIECES
    anywhere, vmem = pl.BlockSpec(memory_space=pl.ANY), pl.BlockSpec(memory_space=pltpu.VMEM)
    smem = pl.BlockSpec(memory_space=pltpu.SMEM)
    dma = pltpu.SemaphoreType.DMA
    bf16, f32 = jnp.bfloat16, jnp.float32
    return pl.pallas_call(
        block_kernel,
        out_shape=(
            jax.ShapeDtypeStruct((tokens, ow), bf16),
            jax.ShapeDtypeStruct((tokens, width), bf16),
            jax.ShapeDtypeStruct((tokens, width), bf16),
        ),
        in_specs=[smem, anywhere, anywhere, anywhere] + [vmem] * 4 + [anywhere] * 2,
        out_specs=(vmem, vmem, vmem),
        scratch_shapes=[
            pltpu.VMEM((tensors, held, features), bf16),
            pltpu.VMEM((tensors, features, wide), bf16),
            pltpu.VMEM((owners * tensors, depth, ow), bf16),
            pltpu.VMEM((tensors, tokens, qw), bf16),
            pltpu.VMEM((tokens, wide), f32),
            pltpu.VMEM((tokens, width), bf16),
            pltpu.VMEM((tokens, width), bf16),
            pltpu.VMEM((2, piece, cache, width), bf16),
            pltpu.VMEM((2, piece, cache, width), bf16),
            pltpu.VMEM((tokens, ow), f32),
            dma((tensors,)),
            dma((2, PIECES)),
            dma((2, PairRing.COPIES)),
            dma((2, CoreShare.COPIES)),
            dma((2, 2, PairRing.COPIES)),
            dma((2,)),
        ],
        compiler_params=pltpu.CompilerParams(
            collective_id=2, has_side_effects=True, vmem_limit_bytes=56 * 1024 * 1024
        ),
        name="decode",
    )(lengths, e_all, w_all, wo_part, q_gain, k_gain, cosine, sine, keys, values)


def requests(ids, vocab_rows, owners):
    count = ids.shape[0]
    owner = ids // vocab_rows
    before = jnp.arange(count)[None, :] < jnp.arange(count)[:, None]
    rank = jnp.sum((owner[:, None] == owner[None, :]) & before, axis=1, dtype=jnp.int32)
    over = jnp.any(rank >= SLOTS).astype(jnp.int32)
    mine = (owner[None, None, :] == jnp.arange(owners)[:, None, None]) & (
        rank[None, None, :] == jnp.arange(SLOTS)[None, :, None]
    )
    wanted = jnp.max(jnp.where(mine, (ids - owner * vocab_rows)[None, None, :], -1), axis=-1)
    rest = jnp.full((owners, LANES - SLOTS), over, jnp.int32)
    asked = jnp.concatenate([wanted, rest], axis=1)
    req = jnp.broadcast_to(asked[:, None, :], (owners, 8, LANES))
    return req, (owner * SLOTS + rank)[:, None]


def all_embeddings(token_ids, embed_table, extra):
    rows, steps = token_ids.shape
    every_id = lax.all_gather(token_ids, "dp", axis=0, tiled=True)
    vocab_rows = embed_table.shape[0]
    local_id = every_id - lax.axis_index("dp") * vocab_rows
    inside = (local_id >= 0) & (local_id < vocab_rows)
    picked = jnp.take(embed_table, jnp.clip(local_id, 0, vocab_rows - 1), axis=0)
    partial_rows = jnp.where(inside[..., None], picked, jnp.zeros((), jnp.bfloat16))
    own = lax.psum_scatter(partial_rows, "dp", scatter_dimension=0, tiled=True)
    own = own.reshape(rows * steps, -1)
    return jnp.concatenate([lax.all_gather(own, "tensor", axis=0, tiled=False), extra], axis=1)


def shards(
    token_ids,
    lengths,
    embed_table,
    norm_gain,
    w_query,
    w_key,
    w_value,
    w_out,
    q_gain,
    k_gain,
    key_cache,
    value_cache,
):
    owners, tensors = lax.axis_size("dp"), lax.axis_size("tensor")
    rows, steps = token_ids.shape
    width = q_gain.shape[0]
    features = embed_table.shape[1]
    req, slot = requests(token_ids.reshape(-1), embed_table.shape[0], owners)
    positions = (lengths[:, None] + jnp.arange(steps, dtype=jnp.int32)[None, :]).reshape(-1)
    half = width // 2
    freq = THETA ** (-jnp.arange(half, dtype=jnp.float32) * 2.0 / width)
    angle = positions.astype(jnp.float32)[:, None] * freq
    cosine, sine = jnp.cos(angle), jnp.sin(angle)
    cosine = jnp.concatenate([cosine, cosine], axis=-1)
    sine = jnp.concatenate([-sine, sine], axis=-1)
    w_all, wo_part, e_all, flag = fetch(
        req, slot, norm_gain[None], embed_table, w_query, w_key, w_value, w_out
    )
    e_all = lax.cond(
        flag[0, 0] > 0,
        lambda kept: all_embeddings(token_ids, embed_table, kept[:, rows * steps:]),
        lambda kept: kept,
        e_all,
    )
    w_all = w_all.reshape(tensors, features, w_all.shape[-1])
    attended, new_keys, new_values = decode(
        lengths, e_all, w_all, wo_part, q_gain[None], k_gain[None],
        cosine, sine, key_cache, value_cache,
    )
    return (
        attended.reshape(rows, steps, -1),
        new_keys.reshape(rows, steps, -1),
        new_values.reshape(rows, steps, -1),
    )


def solution(mesh):
    in_specs = (
        P("dp", None),
        P("dp"),
        P("dp", "tensor"),
        P("tensor"),
        P(("dp", "tensor"), None),
        P(("dp", "tensor"), None),
        P(("dp", "tensor"), None),
        P(("dp", "tensor"), None),
        P(),
        P(),
        P("dp", None, "tensor"),
        P("dp", None, "tensor"),
    )
    out_specs = (P("dp", None, "tensor"), P("dp", None, "tensor"), P("dp", None, "tensor"))
    return jax.shard_map(shards, mesh=mesh, in_specs=in_specs, out_specs=out_specs, check_vma=False)
```

```python
import math

import jax
import jax.numpy as jnp
import numpy as np
from jax import lax
from jax.experimental import pallas as pl
from jax.experimental.pallas import tpu as pltpu
from jax.sharding import PartitionSpec as P

EPS = 1e-06
THETA = 1000000.0
ROWS_AT_ONCE = 4
PIECES = 4
SLOTS = 32
LANES = 128
EXTRA = 16
MESH = pl.DeviceIdType.MESH
NT = (((1,), (1,)), ((), ()))


class Place:
    def __init__(self):
        self.dp = lax.axis_index("dp")
        self.t = lax.axis_index("tensor")
        self.y, self.xh, self.c = self.dp // 4, (self.dp // 2) % 2, self.dp % 2
        self.xl, self.z = self.t // 4, self.t % 4

    def dp_id(self, dy, dxh, dc=0):
        return ((self.y + dy) % 4) * 4 + ((self.xh + dxh) % 2) * 2 + (self.c + dc) % 2

    def t_id(self, dxl, dz):
        return ((self.xl + dxl) % 2) * 4 + (self.z + dz) % 4


def remote(src, dst, sems, k, device):
    return pltpu.make_async_remote_copy(
        src_ref=src,
        dst_ref=dst,
        send_sem=sems.at[0, k],
        recv_sem=sems.at[1, k],
        device_id=device,
        device_id_type=MESH,
    )


def greet(devices):
    barrier = pltpu.get_barrier_semaphore()
    for device in devices:
        pl.semaphore_signal(barrier, inc=1, device_id=device, device_id_type=MESH)
    pl.semaphore_wait(barrier, len(devices))


class PairRing:
    COPIES = 9

    def __init__(self, own, block, first, second, ident, device, sems, landed=None):
        self.landed = landed or (lambda k, e: None)
        self.ident = ident
        pair, nxt, prv = device(0, 1), device(1, 0), device(3, 0)
        me, mate = ident(0, 0), ident(0, 1)
        self.c = [
            remote(own, block(me), sems, 0, pair),
            remote(own, block(me), sems, 1, nxt),
            remote(own, block(me), sems, 2, prv),
            remote(block(mate), block(mate), sems, 3, nxt),
            remote(block(mate), block(mate), sems, 4, prv),
            remote(first(ident(3, 0)), first(ident(3, 0)), sems, 5, nxt),
            remote(second(ident(1, 0)), second(ident(1, 0)), sems, 6, prv),
            remote(first(ident(3, 1)), first(ident(3, 1)), sems, 7, nxt),
            remote(second(ident(1, 1)), second(ident(1, 1)), sems, 8, prv),
        ]

    def s0(self):
        self.c[0].start()
        self.c[1].start()
        self.c[2].start()

    def s1(self):
        self.c[0].wait_recv()
        self.c[3].start()
        self.c[4].start()
        self.landed(0, 1)

    def s2(self):
        self.c[1].wait_recv()
        self.c[5].start()
        self.landed(3, 0)
        self.c[2].wait_recv()
        self.c[6].start()
        self.landed(1, 0)

    def s3(self):
        self.c[3].wait_recv()
        self.c[7].start()
        self.landed(3, 1)
        self.c[4].wait_recv()
        self.c[8].start()
        self.landed(1, 1)

    def s4(self):
        self.c[5].wait_recv()
        self.c[6].wait_recv()
        self.landed(2, 0)
        self.c[7].wait_recv()
        self.c[8].wait_recv()
        self.landed(2, 1)

    def end(self):
        for copy in self.c:
            copy.wait_send()


class RingPair:
    COPIES = 8

    def __init__(self, own, block, first, second, ident, device, sems, landed=None):
        self.landed = landed or (lambda k, e: None)
        pair, nxt, prv = device(0, 1), device(1, 0), device(3, 0)
        me = ident(0, 0)
        self.c = [
            remote(own, block(me), sems, 0, nxt),
            remote(own, block(me), sems, 1, prv),
            remote(first(ident(3, 0)), first(ident(3, 0)), sems, 2, nxt),
            remote(second(ident(1, 0)), second(ident(1, 0)), sems, 3, prv),
            remote(own, block(me), sems, 4, pair),
            remote(block(ident(3, 0)), block(ident(3, 0)), sems, 5, pair),
            remote(block(ident(1, 0)), block(ident(1, 0)), sems, 6, pair),
            remote(block(ident(2, 0)), block(ident(2, 0)), sems, 7, pair),
        ]

    def s0(self):
        self.c[0].start()
        self.c[1].start()
        self.c[4].start()

    def s1(self):
        self.c[0].wait_recv()
        self.c[2].start()
        self.c[5].start()
        self.landed(3, 0)
        self.c[1].wait_recv()
        self.c[3].start()
        self.c[6].start()
        self.landed(1, 0)

    def s2(self):
        self.c[2].wait_recv()
        self.c[3].wait_recv()
        self.c[7].start()
        self.landed(2, 0)

    def s3(self):
        self.c[4].wait_recv()
        self.landed(0, 1)
        self.c[5].wait_recv()
        self.landed(3, 1)
        self.c[6].wait_recv()
        self.landed(1, 1)

    def s4(self):
        self.c[7].wait_recv()
        self.landed(2, 1)

    def end(self):
        for copy in self.c:
            copy.wait_send()


class CoreShare:
    COPIES = 8

    def __init__(self, block, place, sems):
        self.block, self.place, self.sems = block, place, sems
        self.copies = {}

    def give(self, src, k, e):
        p = self.place
        copy = remote(
            src, self.block(p.dp_id(k, e)), self.sems, k * 2 + e, (p.dp_id(0, 0, 1), p.t)
        )
        copy.start()
        self.copies[k, e] = copy

    def took(self, k, e):
        self.copies[k, e].wait_recv()

    def end(self):
        for copy in self.copies.values():
            copy.wait_send()


class Columns:
    def __init__(self, own, blocks, count, place, ring_sems, share_sems):
        cut = count * 3 // 4
        rest = count - cut

        def made(kind, start, size, sems, share_sems):
            half = size // 2
            block = lambda i: blocks(i, start, size)
            share = CoreShare(block, place, share_sems)
            ring = kind(
                own(start, size),
                block,
                lambda i: blocks(i, start, half),
                lambda i: blocks(i, start + half, size - half),
                place.dp_id,
                lambda k, e: (place.dp_id(k, e), place.t),
                sems,
                lambda k, e: share.give(block(place.dp_id(k, e)), k, e),
            )
            return ring, share

        self.a, self.share_a = made(PairRing, 0, cut, ring_sems.at[0], share_sems.at[0])
        self.b, self.share_b = made(RingPair, cut, rest, ring_sems.at[1], share_sems.at[1])
        self.mine_a, self.mine_b = own(0, cut), own(cut, rest)

    def s0(self):
        self.a.s0()
        self.b.s0()
        self.share_a.give(self.mine_a, 0, 0)
        self.share_b.give(self.mine_b, 0, 0)

    def took(self, k, e):
        self.share_a.took(k, e)
        self.share_b.took(k, e)

    def end(self):
        self.a.end()
        self.b.end()
        self.share_a.end()
        self.share_b.end()


AROUND = ((0, 0), (0, 1), (1, 0), (3, 0), (1, 1), (3, 1), (2, 0), (2, 1))


def step_kernel(
    lengths, req, slot, gain, table, wq, wk, wv, wo, q_gain, k_gain, cosine, sine, key_cache, value_cache,
    attended, new_keys, new_values, flag, wa_all, wb_all,
    reqs, slot_v, gain_v, cos_v, sin_v, index_v, slots_out, slots_in, e_own, e_v, n_v, square_v,
    wa_v, wb_v, wo_part, wo_v, heads_v, acc_a, acc_b, nk_v, nv_v, k_v, v_v, total_v,
    req_sems, slot_sems, p1_sems, o1_sems, ring_sems, share_sems,
    e_sems, heads_sems, load_sems, kv_sems, local_sems,
):
    p = Place()
    dp, t = p.dp, p.t
    owners, tensors = reqs.shape[0], e_v.shape[0]
    tokens, features = attended.shape[0], e_v.shape[2]
    vocab = table.shape[0]
    height = wq.shape[0]
    width = LANES
    rows, cache = key_cache.shape[0], key_cache.shape[1]
    steps = tokens // rows
    qw, kw = wq.shape[1] // tensors, wk.shape[1] // tensors
    ow = wo.shape[1] // tensors
    heads = qw // width
    dp_peers = [(lax.rem(dp + j, owners), t) for j in range(1, owners)]
    t_peers = [(dp, lax.rem(t + j, tensors)) for j in range(1, tensors)]
    greet(dp_peers + t_peers)

    asks = []
    for j in range(1, owners):
        to = lax.rem(dp + j, owners)
        copy = remote(req.at[to], reqs.at[dp], req_sems, j, (to, t))
        copy.start()
        asks.append(copy)
    own_ask = pltpu.make_async_copy(req.at[dp], reqs.at[dp], local_sems.at[0])
    own_ask.start()

    stored = pl.ds(pl.multiple_of((dp * tensors + t) * height, 8), height)
    hw = qw // 2
    parts = (
        (wq, qw, 0, hw, wa_all, 0),
        (wk, kw, 0, kw, wa_all, hw),
        (wv, kw, 0, kw, wa_all, hw + kw),
        (wq, qw, hw, hw, wb_all, 0),
    )

    def columns_of(w, whole, at, n, to):
        return w.at[:, pl.ds(pl.multiple_of(to * whole + at, LANES), n)]

    first = ([], [])
    for half, some in enumerate((parts[:3], parts[3:])):
        for j in range(1, tensors):
            to = lax.rem(t + j, tensors)
            for a, (w, whole, at, n, into, column) in enumerate(some):
                copy = remote(
                    columns_of(w, whole, at, n, to),
                    into.at[stored, pl.ds(column, n)],
                    p1_sems, j * 4 + half * 3 + a, (dp, to),
                )
                copy.start()
                first[half].append(copy)
        if half == 0:
            load_table = pltpu.make_async_copy(
                table, wa_v.at[pl.ds(0, vocab), pl.ds(0, features)], local_sems.at[1]
            )
            load_table.start()
    stays = [
        pltpu.make_async_copy(
            columns_of(w, whole, at, n, t), into.at[stored, pl.ds(column, n)], local_sems.at[13 + a]
        )
        for a, (w, whole, at, n, into, column) in enumerate(parts)
    ]
    stays.append(
        pltpu.make_async_copy(
            wo.at[:, pl.ds(pl.multiple_of(t * ow, LANES), ow)], wo_part.at[t], local_sems.at[5]
        )
    )
    small = [
        pltpu.make_async_copy(a, b, local_sems.at[6 + i])
        for i, (a, b) in enumerate(((slot, slot_v), (gain, gain_v), (cosine, cos_v), (sine, sin_v)))
    ]
    for copy in stays + small:
        copy.start()

    padded = -(-vocab // LANES) * LANES
    wa_v[pl.ds(vocab, padded - vocab), pl.ds(0, features)] = jnp.zeros(
        (padded - vocab, features), wa_v.dtype
    )
    for copy in asks:
        copy.wait_recv()
    own_ask.wait()
    asked = jnp.concatenate(
        [reqs[lax.rem(dp + j, owners), 0:1, :] for j in range(owners)], axis=0
    )
    over = jnp.max(jnp.where(lax.broadcasted_iota(jnp.int32, asked.shape, 1) == SLOTS, asked, 0))
    flag[0, 0] = over
    columns = jnp.transpose(asked)
    for j in range(owners):
        index_v[j * SLOTS:(j + 1) * SLOTS, :] = jnp.broadcast_to(
            columns[:SLOTS, j:j + 1], (SLOTS, LANES)
        )
    load_table.wait()

    def columns(own, block, n):
        return Columns(own, block, tensors, p, ring_sems.at[n], share_sems.at[n])

    def in_projection(ref, n):
        def block(i, at, size):
            start = pl.multiple_of((i * tensors + at) * height, 8)
            return ref.at[pl.ds(start, size * height)]

        return columns(lambda at, size: block(dp, at, size), block, n)

    cols_a = in_projection(wa_all, 0)
    cols_b = in_projection(wb_all, 1)
    outs = columns(
        lambda at, size: wo_part.at[pl.ds(at, size)],
        lambda i, at, size: wo_v.at[pl.ds(i * tensors + at, size)],
        2,
    )

    chunk = 8
    replies = []
    for m in range(owners // chunk):
        wanted = index_v[m * chunk * SLOTS:(m + 1) * chunk * SLOTS, 0:1]
        place = lax.broadcasted_iota(jnp.int32, (chunk * SLOTS, padded), 1)
        hit = (place == wanted).astype(jnp.float32).astype(jnp.bfloat16)
        picked = jnp.dot(
            hit, wa_v[0:padded, 0:features], preferred_element_type=jnp.float32
        )
        slots_out[m * chunk:(m + 1) * chunk] = picked.astype(jnp.bfloat16).reshape(
            chunk, SLOTS, features
        )
        for j in range(m * chunk, (m + 1) * chunk):
            if j == 0:
                copy = pltpu.make_async_copy(slots_out.at[0], slots_in.at[dp], local_sems.at[10])
            else:
                copy = remote(
                    slots_out.at[j], slots_in.at[dp], slot_sems, j, (lax.rem(dp + j, owners), t)
                )
            copy.start()
            replies.append(copy)

    for copy in first[0]:
        copy.wait_recv()
    for copy in stays:
        copy.wait()
    cols_a.s0()
    second = []
    for j in range(1, tensors):
        to = lax.rem(t + j, tensors)
        copy = remote(
            wo.at[:, pl.ds(pl.multiple_of(to * ow, LANES), ow)],
            wo_part.at[t],
            o1_sems, j, (dp, to),
        )
        copy.start()
        second.append(copy)

    piece = rows // PIECES

    def load_kv(n):
        i = n % PIECES
        at = pl.ds(i * piece, piece)
        return (
            pltpu.make_async_copy(key_cache.at[at], k_v.at[i % 2], kv_sems.at[0, n]),
            pltpu.make_async_copy(value_cache.at[at], v_v.at[i % 2], kv_sems.at[1, n]),
        )

    caches = [load_kv(n) for n in range(2 * PIECES)]
    for copy in caches[0] + caches[1]:
        copy.start()

    for copy in small:
        copy.wait()
    replies[0].wait()
    for copy in replies[1:]:
        copy.wait_recv()
    slots_of = jnp.transpose(slot_v[...])[:, 0:1]
    picks = lax.broadcasted_iota(jnp.int32, (tokens, owners * SLOTS), 1) == slots_of
    e_own[0:tokens] = jnp.dot(
        picks.astype(jnp.float32).astype(jnp.bfloat16),
        slots_in[...].reshape(owners * SLOTS, features),
        preferred_element_type=jnp.float32,
    ).astype(jnp.bfloat16)
    e_own[tokens:] = gain_v[...]
    e_ring = PairRing(
        e_own,
        lambda i: e_v.at[i],
        lambda i: e_v.at[i, pl.ds(0, tokens // 2)],
        lambda i: e_v.at[i, pl.ds(tokens // 2, tokens // 2 + EXTRA)],
        lambda k, e: p.t_id(e, k),
        lambda k, e: (dp, p.t_id(e, k)),
        e_sems,
    )
    e_ring.s0()
    keep_e = pltpu.make_async_copy(e_own, e_v.at[t], local_sems.at[11])
    keep_e.start()

    def square(ref):
        wide = ref[...].astype(jnp.float32)
        wide = wide * wide
        part = wide[:, 0:LANES]
        for i in range(1, features // LANES):
            part = part + wide[:, i * LANES:(i + 1) * LANES]
        return part

    def add_square(k, e):
        square_v[...] = square_v[...] + square(e_v.at[p.t_id(e, k), pl.ds(0, tokens)])

    cols_a.a.s1()
    cols_a.b.s1()
    square_v[...] = square(e_own.at[pl.ds(0, tokens)])
    e_ring.s1()
    add_square(0, 1)
    cols_a.a.s2()
    cols_a.b.s2()
    e_ring.s2()
    add_square(3, 0)
    add_square(1, 0)
    cols_a.a.s3()
    for copy in first[1]:
        copy.wait_recv()
    cols_b.s0()
    e_ring.s3()
    add_square(3, 1)
    add_square(1, 1)

    part = tensors * height
    loads = {}

    def load_all(cols, ref, into, n, places):
        for k, e in places:
            for dc in (0, 1):
                if dc:
                    cols.took(k, e)
                at = pl.multiple_of(p.dp_id(k, e, dc) * part, part)
                loads[n, k, e, dc] = pltpu.make_async_copy(
                    ref.at[pl.ds(at, part)],
                    into.at[pl.ds(at, part)],
                    load_sems.at[n, dc, k * 2 + e],
                )
                loads[n, k, e, dc].start()

    def loaded(n, places):
        for k, e in places:
            loads[n, k, e, 0].wait()
            loads[n, k, e, 1].wait()

    cols_a.b.s3()
    load_all(cols_a, wa_all, wa_v, 0, AROUND[:6])
    e_ring.s4()
    keep_e.wait()
    add_square(2, 0)
    add_square(2, 1)

    total = jnp.sum(square_v[...], axis=-1, keepdims=True)
    inverse = lax.rsqrt(total / (tensors * features) + EPS)

    def norm(i, carry):
        weight = e_v[i, pl.ds(tokens, EXTRA)].astype(jnp.float32)[0:1]
        normed = e_v[i, pl.ds(0, tokens)].astype(jnp.float32) * inverse * weight
        n_v[i] = normed.astype(jnp.bfloat16)
        return carry

    lax.fori_loop(0, tensors, norm, 0)

    def project(into, w, k, e):
        i = lax.div(p.dp_id(k, e), 2)
        into[...] = into[...] + jnp.dot(
            n_v[i],
            w[pl.ds(pl.multiple_of(i * 2 * part, 2 * part), 2 * part), :],
            preferred_element_type=jnp.float32,
        )

    def project_all(cols, ref, w, into, n):
        def early(j, carry):
            k = lax.div(j, 2)
            project(into, w, jnp.where(k == 2, 3, k), lax.rem(j, 2))
            return carry

        def late(j, carry):
            project(into, w, 2, j)
            return carry

        into[...] = jnp.zeros(into.shape, jnp.float32)
        loaded(n, AROUND[:6])
        lax.fori_loop(0, 6, early, 0)
        cols.a.s4()
        cols.b.s4()
        load_all(cols, ref, w, n, AROUND[6:])
        loaded(n, AROUND[6:])
        lax.fori_loop(0, 2, late, 0)

    cols_b.a.s1()
    cols_b.b.s1()
    project_all(cols_a, wa_all, wa_v, acc_a, 0)
    cols_b.a.s2()
    cols_b.b.s2()

    def placed(raw, head_gain):
        mean_sq = jnp.mean(raw * raw, axis=-1, keepdims=True)
        scaled = raw * lax.rsqrt(mean_sq + EPS) * head_gain
        return scaled * cos_v[...] + pltpu.roll(scaled, width // 2, 1) * sin_v[...]

    head_gain = q_gain[...].astype(jnp.float32)

    def place_heads(acc):
        for h in range(heads // 2):
            at = slice(h * width, (h + 1) * width)
            acc[:, at] = placed(acc[:, at], head_gain)

    place_heads(acc_a)
    nk_v[...] = placed(acc_a[:, hw:hw + kw], k_gain[...].astype(jnp.float32)).astype(jnp.bfloat16)
    nv_v[...] = acc_a[:, hw + kw:hw + 2 * kw].astype(jnp.bfloat16)
    new_keys[...] = nk_v[...]
    new_values[...] = nv_v[...]

    scale = 1.0 / math.sqrt(width)
    pair = 2 * steps
    group = ROWS_AT_ONCE * steps
    some = heads // 2
    query = lax.broadcasted_iota(jnp.int32, (some * pair, 1), 0) % pair
    is_first = query < steps
    fresh = lax.broadcasted_iota(jnp.int32, (some * pair, group), 1)
    column = lax.broadcasted_iota(jnp.int32, (some * pair, cache), 1)

    def attend(acc, half, i, g):
        at = pl.ds(pl.multiple_of(i * piece * steps + g * group, group), group)
        queries = acc[at, 0:hw]
        keys, values = nk_v[at, :], nv_v[at, :]
        results = []
        for n in range(ROWS_AT_ONCE // 2):
            q = jnp.concatenate(
                [
                    queries[n * pair:(n + 1) * pair, h * width:(h + 1) * width]
                    for h in range(some)
                ],
                axis=0,
            ).astype(jnp.bfloat16)
            r = g * ROWS_AT_ONCE + 2 * n
            old_a = lax.dot_general(q, k_v[i % 2, r], NT, preferred_element_type=jnp.float32)
            old_b = lax.dot_general(q, k_v[i % 2, r + 1], NT, preferred_element_type=jnp.float32)
            new = lax.dot_general(q, keys, NT, preferred_element_type=jnp.float32) * scale
            token = query + n * pair
            new = jnp.where((fresh // steps == token // steps) & (fresh <= token), new, -jnp.inf)
            held = jnp.where(
                is_first, lengths[i * piece + r], lengths[i * piece + r + 1]
            )
            old = jnp.where(is_first, old_a, old_b) * scale
            old = jnp.where(column < held, old, -jnp.inf)
            top = jnp.maximum(
                jnp.max(old, axis=-1, keepdims=True), jnp.max(new, axis=-1, keepdims=True)
            )
            old = jnp.exp(old - top)
            new = jnp.exp(new - top)
            whole = jnp.sum(old, axis=-1, keepdims=True) + jnp.sum(new, axis=-1, keepdims=True)
            inv = 1.0 / whole
            old = (old * inv).astype(jnp.bfloat16)
            new = (new * inv).astype(jnp.bfloat16)
            out_a = jnp.dot(old, v_v[i % 2, r], preferred_element_type=jnp.float32)
            out_b = jnp.dot(old, v_v[i % 2, r + 1], preferred_element_type=jnp.float32)
            out = jnp.where(is_first, out_a, out_b)
            out = out + jnp.dot(new, values, preferred_element_type=jnp.float32)
            results.append(
                jnp.concatenate([out[h * pair:(h + 1) * pair] for h in range(some)], axis=1)
            )
        heads_v[half, t, at, :] = jnp.concatenate(results, axis=0).astype(jnp.bfloat16)

    span = tokens // 2

    def heads_ring(kind, half, at, n, sems):
        return kind(
            heads_v.at[half, t, pl.ds(at, n)],
            lambda i: heads_v.at[half, i, pl.ds(at, n)],
            lambda i: heads_v.at[half, i, pl.ds(at, n // 2)],
            lambda i: heads_v.at[half, i, pl.ds(at + n // 2, n // 2)],
            lambda k, e: p.t_id(e, k),
            lambda k, e: (dp, p.t_id(e, k)),
            sems,
        )

    rings = [
        heads_ring(PairRing, 0, 0, tokens, heads_sems.at[0]),
        heads_ring(PairRing, 1, 0, span, heads_sems.at[1]),
        heads_ring(RingPair, 1, span, span, heads_sems.at[2]),
    ]

    def attend_piece(acc, half, i):
        n = half * PIECES + i
        for copy in caches[n]:
            copy.wait()

        def one(g, carry):
            attend(acc, half, i, g)
            return carry

        lax.fori_loop(0, piece // ROWS_AT_ONCE, one, 0)
        if n + 2 < 2 * PIECES:
            for copy in caches[n + 2]:
                copy.start()

    attend_piece(acc_a, 0, 0)
    cols_b.a.s3()
    for copy in second:
        copy.wait_recv()
    outs.s0()
    keep_o = pltpu.make_async_copy(wo_part, wo_v.at[pl.ds(dp * tensors, tensors)], local_sems.at[12])
    keep_o.start()
    attend_piece(acc_a, 0, 1)
    cols_b.b.s3()
    load_all(cols_b, wb_all, wb_v, 1, AROUND[:6])
    attend_piece(acc_a, 0, 2)
    attend_piece(acc_a, 0, 3)
    rings[0].s0()
    project_all(cols_b, wb_all, wb_v, acc_b, 1)
    outs.a.s1()
    rings[0].s1()
    place_heads(acc_b)
    outs.b.s1()
    attend_piece(acc_b, 1, 0)
    rings[0].s2()
    outs.a.s2()
    attend_piece(acc_b, 1, 1)
    rings[1].s0()
    outs.b.s2()
    rings[0].s3()
    attend_piece(acc_b, 1, 2)
    outs.a.s3()
    rings[1].s1()
    attend_piece(acc_b, 1, 3)
    rings[2].s0()
    rings[1].s2()
    rings[2].s1()
    outs.b.s3()
    rings[1].s3()
    rings[2].s2()
    rings[0].s4()
    outs.a.s4()
    outs.b.s4()
    for k, e in AROUND:
        outs.took(k, e)
    keep_o.wait()

    per = wo_v.shape[0] // tensors // 2
    total_v[...] = e_own[pl.ds(0, tokens)].astype(jnp.float32)

    def back(half):
        def add(i, carry):
            w = wo_v[pl.ds((2 * i + half) * per, per)].reshape(hw, ow)
            total_v[...] = total_v[...] + jnp.dot(
                heads_v[half, i], w, preferred_element_type=jnp.float32
            )
            return carry

        lax.fori_loop(0, tensors, add, 0)

    back(0)
    rings[1].s4()
    rings[2].s3()
    rings[2].s4()
    back(1)
    attended[...] = total_v[...].astype(jnp.bfloat16)
    for copy in first[0] + first[1] + asks + replies[1:] + second:
        copy.wait_send()
    cols_a.end()
    cols_b.end()
    outs.end()
    e_ring.end()
    for ring in rings:
        ring.end()


def step(lengths, req, slot, gain, table, wq, wk, wv, wo, q_gain, k_gain, cosine, sine, keys, values):
    owners, tensors = lax.axis_size("dp"), lax.axis_size("tensor")
    tokens, features = slot.shape[1], table.shape[1]
    rows, cache, width = keys.shape
    height, depth = wq.shape[0], wo.shape[0]
    qw, ow = wq.shape[1] // tensors, wo.shape[1] // tensors
    hw = qw // 2
    piece = rows // PIECES
    anywhere, vmem = pl.BlockSpec(memory_space=pl.ANY), pl.BlockSpec(memory_space=pltpu.VMEM)
    smem = pl.BlockSpec(memory_space=pltpu.SMEM)
    dma = pltpu.SemaphoreType.DMA
    bf16, f32 = jnp.bfloat16, jnp.float32
    return pl.pallas_call(
        step_kernel,
        out_shape=(
            jax.ShapeDtypeStruct((tokens, ow), bf16),
            jax.ShapeDtypeStruct((tokens, width), bf16),
            jax.ShapeDtypeStruct((tokens, width), bf16),
            jax.ShapeDtypeStruct((1, 1), jnp.int32),
            jax.ShapeDtypeStruct((owners * tensors * height, hw + 2 * width), bf16),
            jax.ShapeDtypeStruct((owners * tensors * height, hw), bf16),
        ),
        in_specs=[smem] + [anywhere] * 8 + [vmem] * 2 + [anywhere] * 4,
        out_specs=(vmem, vmem, vmem, smem, anywhere, anywhere),
        scratch_shapes=[
            pltpu.VMEM((owners, 8, LANES), jnp.int32),
            pltpu.VMEM(slot.shape, jnp.int32),
            pltpu.VMEM(gain.shape, bf16),
            pltpu.VMEM(cosine.shape, f32),
            pltpu.VMEM(sine.shape, f32),
            pltpu.VMEM((owners * SLOTS, LANES), jnp.int32),
            pltpu.VMEM((owners, SLOTS, features), bf16),
            pltpu.VMEM((owners, SLOTS, features), bf16),
            pltpu.VMEM((tokens + EXTRA, features), bf16),
            pltpu.VMEM((tensors, tokens + EXTRA, features), bf16),
            pltpu.VMEM((tensors, tokens, features), bf16),
            pltpu.VMEM((tokens, LANES), f32),
            pltpu.VMEM((tensors * features, hw + 2 * width), bf16),
            pltpu.VMEM((tensors * features, hw), bf16),
            pltpu.VMEM((tensors, depth, ow), bf16),
            pltpu.VMEM((owners * tensors, depth, ow), bf16),
            pltpu.VMEM((2, tensors, tokens, hw), bf16),
            pltpu.VMEM((tokens, hw + 2 * width), f32),
            pltpu.VMEM((tokens, hw), f32),
            pltpu.VMEM((tokens, width), bf16),
            pltpu.VMEM((tokens, width), bf16),
            pltpu.VMEM((2, piece, cache, width), bf16),
            pltpu.VMEM((2, piece, cache, width), bf16),
            pltpu.VMEM((tokens, ow), f32),
            dma((2, owners)),
            dma((2, owners)),
            dma((2, 4 * tensors)),
            dma((2, tensors)),
            dma((3, 2, 2, PairRing.COPIES)),
            dma((3, 2, 2, CoreShare.COPIES)),
            dma((2, PairRing.COPIES)),
            dma((3, 2, PairRing.COPIES)),
            dma((2, 2, 8)),
            dma((2, 2 * PIECES)),
            dma((17,)),
        ],
        compiler_params=pltpu.CompilerParams(
            collective_id=1, has_side_effects=True, vmem_limit_bytes=60 * 1024 * 1024
        ),
        name="step",
    )(lengths, req, slot, gain, table, wq, wk, wv, wo, q_gain, k_gain, cosine, sine, keys, values)


def requests(ids, vocab_rows, owners):
    count = ids.shape[0]
    owner = lax.div(ids, jnp.int32(vocab_rows))
    same = ids[:, None] == ids[None, :]
    before = jnp.arange(count)[None, :] < jnp.arange(count)[:, None]
    fresh = ~jnp.any(same & before, axis=1)
    smaller = (owner[:, None] == owner[None, :]) & (ids[None, :] < ids[:, None])
    rank = jnp.sum(smaller & fresh[None, :], axis=1, dtype=jnp.int32)
    over = jnp.any(rank >= SLOTS).astype(jnp.int32)
    mine = (owner[None, None, :] == jnp.arange(owners)[:, None, None]) & (
        rank[None, None, :] == jnp.arange(SLOTS)[None, :, None]
    )
    wanted = jnp.max(jnp.where(mine, (ids - owner * vocab_rows)[None, None, :], -1), axis=-1)
    rest = jnp.full((owners, LANES - SLOTS), over, jnp.int32)
    asked = jnp.concatenate([wanted, rest], axis=1)
    req = jnp.broadcast_to(asked[:, None, :], (owners, 8, LANES))
    return req, jnp.broadcast_to((owner * SLOTS + rank)[None, :], (8, count))


def rms_scale(values, gain):
    mean_sq = jnp.mean(values * values, axis=-1, keepdims=True)
    return values * lax.rsqrt(mean_sq + EPS) * gain.astype(jnp.float32)


def rotate(values, positions):
    half = values.shape[-1] // 2
    freq = THETA ** (-jnp.arange(half, dtype=jnp.float32) * 2.0 / values.shape[-1])
    angle = positions.astype(jnp.float32)[:, :, None, None] * freq
    cosine = jnp.cos(angle)
    sine = jnp.sin(angle)
    first = values[..., :half]
    second = values[..., half:]
    return jnp.concatenate(
        [first * cosine - second * sine, second * cosine + first * sine], axis=-1
    )


def attend(query, fresh_keys, fresh_values, key_cache, value_cache, lengths):
    rows, steps, heads_count, width = query.shape
    kv_heads = fresh_keys.shape[2]
    group = heads_count // kv_heads
    cache_len = key_cache.shape[1]
    grouped = query.reshape(rows, steps, kv_heads, group, width)
    keys = key_cache.reshape(rows, cache_len, kv_heads, width)
    values = value_cache.reshape(rows, cache_len, kv_heads, width)
    scale = 1.0 / math.sqrt(width)
    old_scores = (
        jnp.einsum("rskgd,rckd->rkgsc", grouped, keys, preferred_element_type=jnp.float32) * scale
    )
    new_scores = (
        jnp.einsum("rskgd,rtkd->rkgst", grouped, fresh_keys, preferred_element_type=jnp.float32)
        * scale
    )
    valid = jnp.arange(cache_len)[None, :] < lengths[:, None]
    old_scores = jnp.where(valid[:, None, None, None, :], old_scores, -jnp.inf)
    causal = jnp.arange(steps)[None, :] <= jnp.arange(steps)[:, None]
    new_scores = jnp.where(causal[None, None, None, :, :], new_scores, -jnp.inf)
    highest = jnp.maximum(jnp.max(old_scores, axis=-1), jnp.max(new_scores, axis=-1))
    old_exp = jnp.exp(old_scores - highest[..., None])
    new_exp = jnp.exp(new_scores - highest[..., None])
    total = jnp.sum(old_exp, axis=-1) + jnp.sum(new_exp, axis=-1)
    old_weights = (old_exp / total[..., None]).astype(jnp.bfloat16)
    new_weights = (new_exp / total[..., None]).astype(jnp.bfloat16)
    mixed = jnp.einsum("rkgsc,rckd->rskgd", old_weights, values, preferred_element_type=jnp.float32)
    mixed = mixed + jnp.einsum(
        "rkgst,rtkd->rskgd", new_weights, fresh_values, preferred_element_type=jnp.float32
    )
    return mixed.reshape(rows, steps, heads_count * width).astype(jnp.bfloat16)


def owned_columns(local):
    half = lax.all_to_all(local, "tensor", split_axis=1, concat_axis=0, tiled=True)
    return lax.all_gather(half, "dp", axis=0, tiled=True)


def plain(
    token_ids, lengths, embed_table, norm_gain, w_query, w_key, w_value, w_out, q_gain, k_gain, key_cache, value_cache
):
    rows, steps = token_ids.shape
    width = q_gain.shape[0]
    every_id = lax.all_gather(token_ids, "dp", axis=0, tiled=True)
    vocab_rows = embed_table.shape[0]
    local_id = every_id - lax.axis_index("dp") * vocab_rows
    inside = (local_id >= 0) & (local_id < vocab_rows)
    picked = jnp.take(embed_table, jnp.clip(local_id, 0, vocab_rows - 1), axis=0)
    partial_rows = jnp.where(inside[..., None], picked, jnp.zeros((), jnp.bfloat16))
    own_rows = lax.psum_scatter(partial_rows, "dp", scatter_dimension=0, tiled=True)
    whole = lax.all_gather(own_rows, "tensor", axis=2, tiled=True)
    gain_full = lax.all_gather(norm_gain, "tensor", axis=0, tiled=True)
    normed = rms_scale(whole.astype(jnp.float32), gain_full).astype(jnp.bfloat16)
    flat = normed.reshape(rows * steps, -1)
    wq = owned_columns(w_query)
    wk = owned_columns(w_key)
    wv = owned_columns(w_value)
    wo = owned_columns(w_out)
    query_raw = jnp.dot(flat, wq, preferred_element_type=jnp.float32)
    key_raw = jnp.dot(flat, wk, preferred_element_type=jnp.float32)
    value_raw = jnp.dot(flat, wv, preferred_element_type=jnp.float32)
    positions = lengths[:, None] + jnp.arange(steps, dtype=jnp.int32)[None, :]
    query_raw = query_raw.reshape(rows, steps, -1, width)
    key_raw = key_raw.reshape(rows, steps, -1, width)
    fresh_values = value_raw.astype(jnp.bfloat16).reshape(rows, steps, -1, width)
    query = rotate(rms_scale(query_raw, q_gain), positions).astype(jnp.bfloat16)
    fresh_keys = rotate(rms_scale(key_raw, k_gain), positions).astype(jnp.bfloat16)
    local_heads = attend(query, fresh_keys, fresh_values, key_cache, value_cache, lengths)
    all_heads = lax.all_gather(local_heads, "tensor", axis=2, tiled=True).reshape(rows * steps, -1)
    projected = jnp.dot(all_heads, wo, preferred_element_type=jnp.float32)
    output = projected + own_rows.astype(jnp.float32).reshape(rows * steps, -1)
    attended = output.astype(jnp.bfloat16).reshape(rows, steps, -1)
    return (attended, fresh_keys.reshape(rows, steps, -1), fresh_values.reshape(rows, steps, -1))


def shards(
    token_ids,
    lengths,
    embed_table,
    norm_gain,
    w_query,
    w_key,
    w_value,
    w_out,
    q_gain,
    k_gain,
    key_cache,
    value_cache,
):
    owners = lax.axis_size("dp")
    rows, steps = token_ids.shape
    width = q_gain.shape[0]
    req, slot = requests(token_ids.reshape(-1), embed_table.shape[0], owners)
    positions = lengths[:, None] + jnp.arange(steps, dtype=jnp.int32)[None, :]
    half = width // 2
    freq = THETA ** (-(np.arange(width) % half) * 2.0 / width)
    angle = positions.astype(jnp.float32)[:, :, None] * freq.astype(np.float32)
    sign = np.where(np.arange(width) < half, -1.0, 1.0).astype(np.float32)
    cosine = jnp.cos(angle).reshape(rows * steps, width)
    sine = (jnp.sin(angle) * sign).reshape(rows * steps, width)
    attended, new_keys, new_values, flag, _, _ = step(
        lengths, req, slot, jnp.broadcast_to(norm_gain[None], (EXTRA, norm_gain.shape[0])), embed_table, w_query, w_key, w_value, w_out,
        q_gain[None], k_gain[None], cosine, sine, key_cache, value_cache,
    )
    given = (
        token_ids, lengths, embed_table, norm_gain, w_query, w_key, w_value, w_out, q_gain, k_gain,
        key_cache, value_cache,
    )
    return lax.cond(
        flag[0, 0] > 0,
        lambda: plain(*given),
        lambda: (
            attended.reshape(rows, steps, -1),
            new_keys.reshape(rows, steps, -1),
            new_values.reshape(rows, steps, -1),
        ),
    )


def solution(mesh):
    in_specs = (
        P("dp", None),
        P("dp"),
        P("dp", "tensor"),
        P("tensor"),
        P(("dp", "tensor"), None),
        P(("dp", "tensor"), None),
        P(("dp", "tensor"), None),
        P(("dp", "tensor"), None),
        P(),
        P(),
        P("dp", None, "tensor"),
        P("dp", None, "tensor"),
    )
    out_specs = (P("dp", None, "tensor"), P("dp", None, "tensor"), P("dp", None, "tensor"))
    return jax.shard_map(shards, mesh=mesh, in_specs=in_specs, out_specs=out_specs, check_vma=False)
```

```python
import math

import jax
import jax.numpy as jnp
import numpy as np
from jax import lax
from jax.experimental import pallas as pl
from jax.experimental.pallas import tpu as pltpu
from jax.sharding import PartitionSpec as P

EPS = 1e-06
THETA = 1000000.0
ROWS_AT_ONCE = 8
PIECES = 4
SLOTS = 32
LANES = 128
EXTRA = 16
MESH = pl.DeviceIdType.MESH
NT = (((1,), (1,)), ((), ()))


class Place:
    def __init__(self):
        self.dp = lax.axis_index("dp")
        self.t = lax.axis_index("tensor")
        self.y, self.xh, self.c = self.dp // 4, (self.dp // 2) % 2, self.dp % 2
        self.xl, self.z = self.t // 4, self.t % 4

    def dp_id(self, dy, dxh, dc=0):
        return ((self.y + dy) % 4) * 4 + ((self.xh + dxh) % 2) * 2 + (self.c + dc) % 2

    def t_id(self, dxl, dz):
        return ((self.xl + dxl) % 2) * 4 + (self.z + dz) % 4


def remote(src, dst, sems, k, device):
    return pltpu.make_async_remote_copy(
        src_ref=src,
        dst_ref=dst,
        send_sem=sems.at[0, k],
        recv_sem=sems.at[1, k],
        device_id=device,
        device_id_type=MESH,
    )


def greet(devices):
    barrier = pltpu.get_barrier_semaphore()
    for device in devices:
        pl.semaphore_signal(barrier, inc=1, device_id=device, device_id_type=MESH)
    pl.semaphore_wait(barrier, len(devices))


class PairRing:
    COPIES = 9

    def __init__(self, own, block, first, second, ident, device, sems, landed=None):
        self.landed = landed or (lambda k, e: None)
        self.ident = ident
        pair, nxt, prv = device(0, 1), device(1, 0), device(3, 0)
        me, mate = ident(0, 0), ident(0, 1)
        self.c = [
            remote(own, block(me), sems, 0, pair),
            remote(own, block(me), sems, 1, nxt),
            remote(own, block(me), sems, 2, prv),
            remote(block(mate), block(mate), sems, 3, nxt),
            remote(block(mate), block(mate), sems, 4, prv),
            remote(first(ident(3, 0)), first(ident(3, 0)), sems, 5, nxt),
            remote(second(ident(1, 0)), second(ident(1, 0)), sems, 6, prv),
            remote(first(ident(3, 1)), first(ident(3, 1)), sems, 7, nxt),
            remote(second(ident(1, 1)), second(ident(1, 1)), sems, 8, prv),
        ]

    def s0(self):
        self.c[0].start()
        self.c[1].start()
        self.c[2].start()

    def s1(self):
        self.c[0].wait_recv()
        self.c[3].start()
        self.c[4].start()
        self.landed(0, 1)

    def s2(self):
        self.c[1].wait_recv()
        self.c[5].start()
        self.landed(3, 0)
        self.c[2].wait_recv()
        self.c[6].start()
        self.landed(1, 0)

    def s3(self):
        self.c[3].wait_recv()
        self.c[7].start()
        self.landed(3, 1)
        self.c[4].wait_recv()
        self.c[8].start()
        self.landed(1, 1)

    def s4(self):
        self.c[5].wait_recv()
        self.c[6].wait_recv()
        self.landed(2, 0)
        self.c[7].wait_recv()
        self.c[8].wait_recv()
        self.landed(2, 1)

    def end(self):
        for copy in self.c:
            copy.wait_send()


class RingPair:
    COPIES = 8

    def __init__(self, own, block, first, second, ident, device, sems, landed=None):
        self.landed = landed or (lambda k, e: None)
        pair, nxt, prv = device(0, 1), device(1, 0), device(3, 0)
        me = ident(0, 0)
        self.c = [
            remote(own, block(me), sems, 0, nxt),
            remote(own, block(me), sems, 1, prv),
            remote(first(ident(3, 0)), first(ident(3, 0)), sems, 2, nxt),
            remote(second(ident(1, 0)), second(ident(1, 0)), sems, 3, prv),
            remote(own, block(me), sems, 4, pair),
            remote(block(ident(3, 0)), block(ident(3, 0)), sems, 5, pair),
            remote(block(ident(1, 0)), block(ident(1, 0)), sems, 6, pair),
            remote(block(ident(2, 0)), block(ident(2, 0)), sems, 7, pair),
        ]

    def s0(self):
        self.c[0].start()
        self.c[1].start()
        self.c[4].start()

    def s1(self):
        self.c[0].wait_recv()
        self.c[2].start()
        self.c[5].start()
        self.landed(3, 0)
        self.c[1].wait_recv()
        self.c[3].start()
        self.c[6].start()
        self.landed(1, 0)

    def s2(self):
        self.c[2].wait_recv()
        self.c[3].wait_recv()
        self.c[7].start()
        self.landed(2, 0)

    def s3(self):
        self.c[4].wait_recv()
        self.landed(0, 1)
        self.c[5].wait_recv()
        self.landed(3, 1)
        self.c[6].wait_recv()
        self.landed(1, 1)

    def s4(self):
        self.c[7].wait_recv()
        self.landed(2, 1)

    def end(self):
        for copy in self.c:
            copy.wait_send()


class CoreShare:
    COPIES = 8

    def __init__(self, block, place, sems):
        self.block, self.place, self.sems = block, place, sems
        self.copies = {}

    def give(self, src, k, e):
        p = self.place
        copy = remote(
            src, self.block(p.dp_id(k, e)), self.sems, k * 2 + e, (p.dp_id(0, 0, 1), p.t)
        )
        copy.start()
        self.copies[k, e] = copy

    def took(self, k, e):
        self.copies[k, e].wait_recv()

    def end(self):
        for copy in self.copies.values():
            copy.wait_send()


class Columns:
    def __init__(self, own, blocks, count, place, ring_sems, share_sems):
        cut = count * 3 // 4
        rest = count - cut

        def made(kind, start, size, sems, share_sems):
            half = size // 2
            block = lambda i: blocks(i, start, size)
            share = CoreShare(block, place, share_sems)
            ring = kind(
                own(start, size),
                block,
                lambda i: blocks(i, start, half),
                lambda i: blocks(i, start + half, size - half),
                place.dp_id,
                lambda k, e: (place.dp_id(k, e), place.t),
                sems,
                lambda k, e: share.give(block(place.dp_id(k, e)), k, e),
            )
            return ring, share

        self.a, self.share_a = made(PairRing, 0, cut, ring_sems.at[0], share_sems.at[0])
        self.b, self.share_b = made(RingPair, cut, rest, ring_sems.at[1], share_sems.at[1])
        self.mine_a, self.mine_b = own(0, cut), own(cut, rest)

    def s0(self):
        self.a.s0()
        self.b.s0()
        self.share_a.give(self.mine_a, 0, 0)
        self.share_b.give(self.mine_b, 0, 0)

    def took(self, k, e):
        self.share_a.took(k, e)
        self.share_b.took(k, e)

    def end(self):
        self.a.end()
        self.b.end()
        self.share_a.end()
        self.share_b.end()


AROUND = ((0, 0), (0, 1), (1, 0), (3, 0), (1, 1), (3, 1), (2, 0), (2, 1))


def step_kernel(
    lengths, req, slot, gain, table, wq, wk, wv, wo, q_gain, k_gain, cosine, sine, key_cache, value_cache,
    attended, new_keys, new_values, flag, wa_all, wb_all,
    reqs, slot_v, gain_v, cos_v, sin_v, index_v, slots_out, slots_in, e_own, e_v, n_v, square_v,
    wa_v, wb_v, wo_part, wo_v, heads_v, acc_a, acc_b, nk_v, nv_v, k_v, v_v, total_v,
    req_sems, slot_sems, p1_sems, o1_sems, ring_sems, share_sems,
    e_sems, heads_sems, load_sems, kv_sems, local_sems,
):
    p = Place()
    dp, t = p.dp, p.t
    owners, tensors = reqs.shape[0], e_v.shape[0]
    tokens, features = attended.shape[0], e_v.shape[2]
    vocab = table.shape[0]
    height = wq.shape[0]
    width = LANES
    rows, cache = key_cache.shape[0], key_cache.shape[1]
    steps = tokens // rows
    qw, kw = wq.shape[1] // tensors, wk.shape[1] // tensors
    ow = wo.shape[1] // tensors
    heads = qw // width
    dp_peers = [(lax.rem(dp + j, owners), t) for j in range(1, owners)]
    t_peers = [(dp, lax.rem(t + j, tensors)) for j in range(1, tensors)]
    greet(dp_peers + t_peers)

    asks = []
    for j in range(1, owners):
        to = lax.rem(dp + j, owners)
        copy = remote(req.at[to], reqs.at[dp], req_sems, j, (to, t))
        copy.start()
        asks.append(copy)
    own_ask = pltpu.make_async_copy(req.at[dp], reqs.at[dp], local_sems.at[0])
    own_ask.start()

    stored = pl.ds(pl.multiple_of((dp * tensors + t) * height, 8), height)
    hw = qw // 2
    parts = (
        (wq, qw, 0, hw, wa_all, 0),
        (wk, kw, 0, kw, wa_all, hw),
        (wv, kw, 0, kw, wa_all, hw + kw),
        (wq, qw, hw, hw, wb_all, 0),
    )

    def columns_of(w, whole, at, n, to):
        return w.at[:, pl.ds(pl.multiple_of(to * whole + at, LANES), n)]

    first = ([], [])
    for half, some in enumerate((parts[:3], parts[3:])):
        for j in range(1, tensors):
            to = lax.rem(t + j, tensors)
            for a, (w, whole, at, n, into, column) in enumerate(some):
                copy = remote(
                    columns_of(w, whole, at, n, to),
                    into.at[stored, pl.ds(column, n)],
                    p1_sems, j * 4 + half * 3 + a, (dp, to),
                )
                copy.start()
                first[half].append(copy)
        if half == 0:
            load_table = pltpu.make_async_copy(
                table, wa_v.at[pl.ds(0, vocab), pl.ds(0, features)], local_sems.at[1]
            )
            load_table.start()
    stays = [
        pltpu.make_async_copy(
            columns_of(w, whole, at, n, t), into.at[stored, pl.ds(column, n)], local_sems.at[13 + a]
        )
        for a, (w, whole, at, n, into, column) in enumerate(parts)
    ]
    stays.append(
        pltpu.make_async_copy(
            wo.at[:, pl.ds(pl.multiple_of(t * ow, LANES), ow)], wo_part.at[t], local_sems.at[5]
        )
    )
    small = [
        pltpu.make_async_copy(a, b, local_sems.at[6 + i])
        for i, (a, b) in enumerate(((slot, slot_v), (gain, gain_v), (cosine, cos_v), (sine, sin_v)))
    ]
    for copy in stays + small:
        copy.start()

    padded = -(-vocab // LANES) * LANES
    wa_v[pl.ds(vocab, padded - vocab), pl.ds(0, features)] = jnp.zeros(
        (padded - vocab, features), wa_v.dtype
    )
    for copy in asks:
        copy.wait_recv()
    own_ask.wait()
    asked = jnp.concatenate(
        [reqs[lax.rem(dp + j, owners), 0:1, :] for j in range(owners)], axis=0
    )
    over = jnp.max(jnp.where(lax.broadcasted_iota(jnp.int32, asked.shape, 1) == SLOTS, asked, 0))
    flag[0, 0] = over
    columns = jnp.transpose(asked)
    for j in range(owners):
        index_v[j * SLOTS:(j + 1) * SLOTS, :] = jnp.broadcast_to(
            columns[:SLOTS, j:j + 1], (SLOTS, LANES)
        )
    load_table.wait()

    def columns(own, block, n):
        return Columns(own, block, tensors, p, ring_sems.at[n], share_sems.at[n])

    def in_projection(ref, n):
        def block(i, at, size):
            start = pl.multiple_of((i * tensors + at) * height, 8)
            return ref.at[pl.ds(start, size * height)]

        return columns(lambda at, size: block(dp, at, size), block, n)

    cols_a = in_projection(wa_all, 0)
    cols_b = in_projection(wb_all, 1)
    outs = columns(
        lambda at, size: wo_part.at[pl.ds(at, size)],
        lambda i, at, size: wo_v.at[pl.ds(i * tensors + at, size)],
        2,
    )

    chunk = 8
    replies = []
    for m in range(owners // chunk):
        wanted = index_v[m * chunk * SLOTS:(m + 1) * chunk * SLOTS, 0:1]
        place = lax.broadcasted_iota(jnp.int32, (chunk * SLOTS, padded), 1)
        hit = (place == wanted).astype(jnp.float32).astype(jnp.bfloat16)
        picked = jnp.dot(
            hit, wa_v[0:padded, 0:features], preferred_element_type=jnp.float32
        )
        slots_out[m * chunk:(m + 1) * chunk] = picked.astype(jnp.bfloat16).reshape(
            chunk, SLOTS, features
        )
        for j in range(m * chunk, (m + 1) * chunk):
            if j == 0:
                copy = pltpu.make_async_copy(slots_out.at[0], slots_in.at[dp], local_sems.at[10])
            else:
                copy = remote(
                    slots_out.at[j], slots_in.at[dp], slot_sems, j, (lax.rem(dp + j, owners), t)
                )
            copy.start()
            replies.append(copy)

    for copy in first[0]:
        copy.wait_recv()
    for copy in stays:
        copy.wait()
    cols_a.s0()
    second = []
    for j in range(1, tensors):
        to = lax.rem(t + j, tensors)
        copy = remote(
            wo.at[:, pl.ds(pl.multiple_of(to * ow, LANES), ow)],
            wo_part.at[t],
            o1_sems, j, (dp, to),
        )
        copy.start()
        second.append(copy)

    piece = rows // PIECES

    def load_kv(n):
        i = n % PIECES
        at = pl.ds(i * piece, piece)
        return (
            pltpu.make_async_copy(key_cache.at[at], k_v.at[i % 2], kv_sems.at[0, n]),
            pltpu.make_async_copy(value_cache.at[at], v_v.at[i % 2], kv_sems.at[1, n]),
        )

    caches = [load_kv(n) for n in range(2 * PIECES)]
    for copy in caches[0] + caches[1]:
        copy.start()

    for copy in small:
        copy.wait()
    replies[0].wait()
    for copy in replies[1:]:
        copy.wait_recv()
    slots_of = jnp.transpose(slot_v[...])[:, 0:1]
    picks = lax.broadcasted_iota(jnp.int32, (tokens, owners * SLOTS), 1) == slots_of
    e_own[0:tokens] = jnp.dot(
        picks.astype(jnp.float32).astype(jnp.bfloat16),
        slots_in[...].reshape(owners * SLOTS, features),
        preferred_element_type=jnp.float32,
    ).astype(jnp.bfloat16)
    e_own[tokens:] = gain_v[...]
    e_ring = PairRing(
        e_own,
        lambda i: e_v.at[i],
        lambda i: e_v.at[i, pl.ds(0, tokens // 2)],
        lambda i: e_v.at[i, pl.ds(tokens // 2, tokens // 2 + EXTRA)],
        lambda k, e: p.t_id(e, k),
        lambda k, e: (dp, p.t_id(e, k)),
        e_sems,
    )
    e_ring.s0()
    keep_e = pltpu.make_async_copy(e_own, e_v.at[t], local_sems.at[11])
    keep_e.start()

    def square(ref):
        wide = ref[...].astype(jnp.float32)
        wide = wide * wide
        part = wide[:, 0:LANES]
        for i in range(1, features // LANES):
            part = part + wide[:, i * LANES:(i + 1) * LANES]
        return part

    def add_square(k, e):
        square_v[...] = square_v[...] + square(e_v.at[p.t_id(e, k), pl.ds(0, tokens)])

    cols_a.a.s1()
    cols_a.b.s1()
    square_v[...] = square(e_own.at[pl.ds(0, tokens)])
    e_ring.s1()
    add_square(0, 1)
    cols_a.a.s2()
    cols_a.b.s2()
    e_ring.s2()
    add_square(3, 0)
    add_square(1, 0)
    cols_a.a.s3()
    for copy in first[1]:
        copy.wait_recv()
    cols_b.s0()
    e_ring.s3()
    add_square(3, 1)
    add_square(1, 1)

    part = tensors * height
    loads = {}

    def load_all(cols, ref, into, n, places):
        for k, e in places:
            for dc in (0, 1):
                if dc:
                    cols.took(k, e)
                at = pl.multiple_of(p.dp_id(k, e, dc) * part, part)
                loads[n, k, e, dc] = pltpu.make_async_copy(
                    ref.at[pl.ds(at, part)],
                    into.at[pl.ds(at, part)],
                    load_sems.at[n, dc, k * 2 + e],
                )
                loads[n, k, e, dc].start()

    def loaded(n, places):
        for k, e in places:
            loads[n, k, e, 0].wait()
            loads[n, k, e, 1].wait()

    cols_a.b.s3()
    load_all(cols_a, wa_all, wa_v, 0, AROUND[:6])
    e_ring.s4()
    keep_e.wait()
    add_square(2, 0)
    add_square(2, 1)

    total = jnp.sum(square_v[...], axis=-1, keepdims=True)
    inverse = lax.rsqrt(total / (tensors * features) + EPS)

    def norm(i, carry):
        weight = e_v[i, pl.ds(tokens, EXTRA)].astype(jnp.float32)[0:1]
        normed = e_v[i, pl.ds(0, tokens)].astype(jnp.float32) * inverse * weight
        n_v[i] = normed.astype(jnp.bfloat16)
        return carry

    lax.fori_loop(0, tensors, norm, 0)

    def project(into, w, k, e):
        i = lax.div(p.dp_id(k, e), 2)
        into[...] = into[...] + jnp.dot(
            n_v[i],
            w[pl.ds(pl.multiple_of(i * 2 * part, 2 * part), 2 * part), :],
            preferred_element_type=jnp.float32,
        )

    def project_all(cols, ref, w, into, n):
        def early(j, carry):
            k = lax.div(j, 2)
            project(into, w, jnp.where(k == 2, 3, k), lax.rem(j, 2))
            return carry

        def late(j, carry):
            project(into, w, 2, j)
            return carry

        into[...] = jnp.zeros(into.shape, jnp.float32)
        loaded(n, AROUND[:6])
        lax.fori_loop(0, 6, early, 0)
        cols.a.s4()
        cols.b.s4()
        load_all(cols, ref, w, n, AROUND[6:])
        loaded(n, AROUND[6:])
        lax.fori_loop(0, 2, late, 0)

    cols_b.a.s1()
    cols_b.b.s1()
    project_all(cols_a, wa_all, wa_v, acc_a, 0)
    cols_b.a.s2()
    cols_b.b.s2()

    def placed(raw, head_gain):
        mean_sq = jnp.mean(raw * raw, axis=-1, keepdims=True)
        scaled = raw * lax.rsqrt(mean_sq + EPS) * head_gain
        return scaled * cos_v[...] + pltpu.roll(scaled, width // 2, 1) * sin_v[...]

    head_gain = q_gain[...].astype(jnp.float32)

    def place_heads(acc):
        for h in range(heads // 2):
            at = slice(h * width, (h + 1) * width)
            acc[:, at] = placed(acc[:, at], head_gain)

    place_heads(acc_a)
    nk_v[...] = placed(acc_a[:, hw:hw + kw], k_gain[...].astype(jnp.float32)).astype(jnp.bfloat16)
    nv_v[...] = acc_a[:, hw + kw:hw + 2 * kw].astype(jnp.bfloat16)
    new_keys[...] = nk_v[...]
    new_values[...] = nv_v[...]

    scale = 1.0 / math.sqrt(width)
    pair = 2 * steps
    group = ROWS_AT_ONCE * steps
    some = heads // 2
    count = ROWS_AT_ONCE // 2
    each = some * pair
    index = lax.broadcasted_iota(jnp.int32, (count * each, 1), 0)
    token = index // each * pair + index % pair
    is_first = lax.broadcasted_iota(jnp.int32, (each, 1), 0) % pair < steps
    fresh = lax.broadcasted_iota(jnp.int32, (count * each, group), 1)
    seen = (fresh // steps == token // steps) & (fresh <= token)
    column = lax.broadcasted_iota(jnp.int32, (count * each, cache), 1)
    none = jnp.zeros((each, width), jnp.bfloat16)

    def attend(acc, half, i, g):
        at = pl.ds(pl.multiple_of(i * piece * steps + g * group, group), group)
        queries = acc[at, 0:hw]
        keys, values = nk_v[at, :], nv_v[at, :]
        parts, scores, held = [], [], []
        for n in range(count):
            q = jnp.concatenate(
                [
                    queries[n * pair:(n + 1) * pair, h * width:(h + 1) * width]
                    for h in range(some)
                ],
                axis=0,
            ).astype(jnp.bfloat16)
            parts.append(q)
            r = g * ROWS_AT_ONCE + 2 * n
            wide_q = jnp.concatenate(
                [jnp.where(is_first, q, none), jnp.where(is_first, none, q)], axis=1
            )
            both_k = jnp.concatenate([k_v[i % 2, r], k_v[i % 2, r + 1]], axis=1)
            scores.append(
                lax.dot_general(wide_q, both_k, NT, preferred_element_type=jnp.float32)
            )
            held.append(
                jnp.where(is_first, lengths[i * piece + r], lengths[i * piece + r + 1])
            )
        new = lax.dot_general(
            jnp.concatenate(parts, axis=0), keys, NT, preferred_element_type=jnp.float32
        )
        new = jnp.where(seen, new * scale, -jnp.inf)
        old = jnp.concatenate(scores, axis=0) * scale
        old = jnp.where(column < jnp.concatenate(held, axis=0), old, -jnp.inf)
        top = jnp.maximum(
            jnp.max(old, axis=-1, keepdims=True), jnp.max(new, axis=-1, keepdims=True)
        )
        old = jnp.exp(old - top)
        new = jnp.exp(new - top)
        whole = jnp.sum(old, axis=-1, keepdims=True) + jnp.sum(new, axis=-1, keepdims=True)
        inv = 1.0 / whole
        old = (old * inv).astype(jnp.bfloat16)
        new = (new * inv).astype(jnp.bfloat16)
        out_new = jnp.dot(new, values, preferred_element_type=jnp.float32)
        results = []
        for n in range(count):
            r = g * ROWS_AT_ONCE + 2 * n
            both_v = jnp.concatenate([v_v[i % 2, r], v_v[i % 2, r + 1]], axis=1)
            mine = slice(n * each, (n + 1) * each)
            both = jnp.dot(old[mine], both_v, preferred_element_type=jnp.float32)
            out = jnp.where(is_first, both[:, :width], both[:, width:]) + out_new[mine]
            results.append(
                jnp.concatenate([out[h * pair:(h + 1) * pair] for h in range(some)], axis=1)
            )
        heads_v[half, t, at, :] = jnp.concatenate(results, axis=0).astype(jnp.bfloat16)

    span = tokens // 2

    def heads_ring(kind, half, at, n, sems):
        return kind(
            heads_v.at[half, t, pl.ds(at, n)],
            lambda i: heads_v.at[half, i, pl.ds(at, n)],
            lambda i: heads_v.at[half, i, pl.ds(at, n // 2)],
            lambda i: heads_v.at[half, i, pl.ds(at + n // 2, n // 2)],
            lambda k, e: p.t_id(e, k),
            lambda k, e: (dp, p.t_id(e, k)),
            sems,
        )

    rings = [
        heads_ring(PairRing, 0, 0, tokens, heads_sems.at[0]),
        heads_ring(PairRing, 1, 0, span, heads_sems.at[1]),
        heads_ring(RingPair, 1, span, span, heads_sems.at[2]),
    ]

    def attend_piece(acc, half, i):
        n = half * PIECES + i
        for copy in caches[n]:
            copy.wait()

        def one(g, carry):
            attend(acc, half, i, g)
            return carry

        lax.fori_loop(0, piece // ROWS_AT_ONCE, one, 0)
        if n + 2 < 2 * PIECES:
            for copy in caches[n + 2]:
                copy.start()

    attend_piece(acc_a, 0, 0)
    cols_b.a.s3()
    for copy in second:
        copy.wait_recv()
    outs.s0()
    keep_o = pltpu.make_async_copy(wo_part, wo_v.at[pl.ds(dp * tensors, tensors)], local_sems.at[12])
    keep_o.start()
    attend_piece(acc_a, 0, 1)
    cols_b.b.s3()
    load_all(cols_b, wb_all, wb_v, 1, AROUND[:6])
    attend_piece(acc_a, 0, 2)
    attend_piece(acc_a, 0, 3)
    rings[0].s0()
    project_all(cols_b, wb_all, wb_v, acc_b, 1)
    outs.a.s1()
    rings[0].s1()
    place_heads(acc_b)
    outs.b.s1()
    attend_piece(acc_b, 1, 0)
    rings[0].s2()
    outs.a.s2()
    attend_piece(acc_b, 1, 1)
    rings[1].s0()
    outs.b.s2()
    rings[0].s3()
    attend_piece(acc_b, 1, 2)
    outs.a.s3()
    rings[1].s1()
    attend_piece(acc_b, 1, 3)
    rings[2].s0()
    rings[1].s2()
    rings[2].s1()
    outs.b.s3()
    rings[1].s3()
    rings[2].s2()
    rings[0].s4()
    outs.a.s4()
    outs.b.s4()
    for k, e in AROUND:
        outs.took(k, e)
    keep_o.wait()

    per = wo_v.shape[0] // tensors // 2
    total_v[...] = e_own[pl.ds(0, tokens)].astype(jnp.float32)

    def back(half):
        def add(i, carry):
            w = wo_v[pl.ds((2 * i + half) * per, per)].reshape(hw, ow)
            total_v[...] = total_v[...] + jnp.dot(
                heads_v[half, i], w, preferred_element_type=jnp.float32
            )
            return carry

        lax.fori_loop(0, tensors, add, 0)

    back(0)
    rings[1].s4()
    rings[2].s3()
    rings[2].s4()
    back(1)
    attended[...] = total_v[...].astype(jnp.bfloat16)
    for copy in first[0] + first[1] + asks + replies[1:] + second:
        copy.wait_send()
    cols_a.end()
    cols_b.end()
    outs.end()
    e_ring.end()
    for ring in rings:
        ring.end()


def step(lengths, req, slot, gain, table, wq, wk, wv, wo, q_gain, k_gain, cosine, sine, keys, values):
    owners, tensors = lax.axis_size("dp"), lax.axis_size("tensor")
    tokens, features = slot.shape[1], table.shape[1]
    rows, cache, width = keys.shape
    height, depth = wq.shape[0], wo.shape[0]
    qw, ow = wq.shape[1] // tensors, wo.shape[1] // tensors
    hw = qw // 2
    piece = rows // PIECES
    anywhere, vmem = pl.BlockSpec(memory_space=pl.ANY), pl.BlockSpec(memory_space=pltpu.VMEM)
    smem = pl.BlockSpec(memory_space=pltpu.SMEM)
    dma = pltpu.SemaphoreType.DMA
    bf16, f32 = jnp.bfloat16, jnp.float32
    return pl.pallas_call(
        step_kernel,
        out_shape=(
            jax.ShapeDtypeStruct((tokens, ow), bf16),
            jax.ShapeDtypeStruct((tokens, width), bf16),
            jax.ShapeDtypeStruct((tokens, width), bf16),
            jax.ShapeDtypeStruct((1, 1), jnp.int32),
            jax.ShapeDtypeStruct((owners * tensors * height, hw + 2 * width), bf16),
            jax.ShapeDtypeStruct((owners * tensors * height, hw), bf16),
        ),
        in_specs=[smem] + [anywhere] * 8 + [vmem] * 2 + [anywhere] * 4,
        out_specs=(vmem, vmem, vmem, smem, anywhere, anywhere),
        scratch_shapes=[
            pltpu.VMEM((owners, 8, LANES), jnp.int32),
            pltpu.VMEM(slot.shape, jnp.int32),
            pltpu.VMEM(gain.shape, bf16),
            pltpu.VMEM(cosine.shape, f32),
            pltpu.VMEM(sine.shape, f32),
            pltpu.VMEM((owners * SLOTS, LANES), jnp.int32),
            pltpu.VMEM((owners, SLOTS, features), bf16),
            pltpu.VMEM((owners, SLOTS, features), bf16),
            pltpu.VMEM((tokens + EXTRA, features), bf16),
            pltpu.VMEM((tensors, tokens + EXTRA, features), bf16),
            pltpu.VMEM((tensors, tokens, features), bf16),
            pltpu.VMEM((tokens, LANES), f32),
            pltpu.VMEM((tensors * features, hw + 2 * width), bf16),
            pltpu.VMEM((tensors * features, hw), bf16),
            pltpu.VMEM((tensors, depth, ow), bf16),
            pltpu.VMEM((owners * tensors, depth, ow), bf16),
            pltpu.VMEM((2, tensors, tokens, hw), bf16),
            pltpu.VMEM((tokens, hw + 2 * width), f32),
            pltpu.VMEM((tokens, hw), f32),
            pltpu.VMEM((tokens, width), bf16),
            pltpu.VMEM((tokens, width), bf16),
            pltpu.VMEM((2, piece, cache, width), bf16),
            pltpu.VMEM((2, piece, cache, width), bf16),
            pltpu.VMEM((tokens, ow), f32),
            dma((2, owners)),
            dma((2, owners)),
            dma((2, 4 * tensors)),
            dma((2, tensors)),
            dma((3, 2, 2, PairRing.COPIES)),
            dma((3, 2, 2, CoreShare.COPIES)),
            dma((2, PairRing.COPIES)),
            dma((3, 2, PairRing.COPIES)),
            dma((2, 2, 8)),
            dma((2, 2 * PIECES)),
            dma((17,)),
        ],
        compiler_params=pltpu.CompilerParams(
            collective_id=1, has_side_effects=True, vmem_limit_bytes=60 * 1024 * 1024
        ),
        name="step",
    )(lengths, req, slot, gain, table, wq, wk, wv, wo, q_gain, k_gain, cosine, sine, keys, values)


def requests(ids, vocab_rows, owners):
    count = ids.shape[0]
    owner = lax.div(ids, jnp.int32(vocab_rows))
    same = ids[:, None] == ids[None, :]
    before = jnp.arange(count)[None, :] < jnp.arange(count)[:, None]
    fresh = ~jnp.any(same & before, axis=1)
    smaller = (owner[:, None] == owner[None, :]) & (ids[None, :] < ids[:, None])
    rank = jnp.sum(smaller & fresh[None, :], axis=1, dtype=jnp.int32)
    over = jnp.any(rank >= SLOTS).astype(jnp.int32)
    mine = (owner[None, None, :] == jnp.arange(owners)[:, None, None]) & (
        rank[None, None, :] == jnp.arange(SLOTS)[None, :, None]
    )
    wanted = jnp.max(jnp.where(mine, (ids - owner * vocab_rows)[None, None, :], -1), axis=-1)
    rest = jnp.full((owners, LANES - SLOTS), over, jnp.int32)
    asked = jnp.concatenate([wanted, rest], axis=1)
    req = jnp.broadcast_to(asked[:, None, :], (owners, 8, LANES))
    return req, jnp.broadcast_to((owner * SLOTS + rank)[None, :], (8, count))


def rms_scale(values, gain):
    mean_sq = jnp.mean(values * values, axis=-1, keepdims=True)
    return values * lax.rsqrt(mean_sq + EPS) * gain.astype(jnp.float32)


def rotate(values, positions):
    half = values.shape[-1] // 2
    freq = THETA ** (-jnp.arange(half, dtype=jnp.float32) * 2.0 / values.shape[-1])
    angle = positions.astype(jnp.float32)[:, :, None, None] * freq
    cosine = jnp.cos(angle)
    sine = jnp.sin(angle)
    first = values[..., :half]
    second = values[..., half:]
    return jnp.concatenate(
        [first * cosine - second * sine, second * cosine + first * sine], axis=-1
    )


def attend(query, fresh_keys, fresh_values, key_cache, value_cache, lengths):
    rows, steps, heads_count, width = query.shape
    kv_heads = fresh_keys.shape[2]
    group = heads_count // kv_heads
    cache_len = key_cache.shape[1]
    grouped = query.reshape(rows, steps, kv_heads, group, width)
    keys = key_cache.reshape(rows, cache_len, kv_heads, width)
    values = value_cache.reshape(rows, cache_len, kv_heads, width)
    scale = 1.0 / math.sqrt(width)
    old_scores = (
        jnp.einsum("rskgd,rckd->rkgsc", grouped, keys, preferred_element_type=jnp.float32) * scale
    )
    new_scores = (
        jnp.einsum("rskgd,rtkd->rkgst", grouped, fresh_keys, preferred_element_type=jnp.float32)
        * scale
    )
    valid = jnp.arange(cache_len)[None, :] < lengths[:, None]
    old_scores = jnp.where(valid[:, None, None, None, :], old_scores, -jnp.inf)
    causal = jnp.arange(steps)[None, :] <= jnp.arange(steps)[:, None]
    new_scores = jnp.where(causal[None, None, None, :, :], new_scores, -jnp.inf)
    highest = jnp.maximum(jnp.max(old_scores, axis=-1), jnp.max(new_scores, axis=-1))
    old_exp = jnp.exp(old_scores - highest[..., None])
    new_exp = jnp.exp(new_scores - highest[..., None])
    total = jnp.sum(old_exp, axis=-1) + jnp.sum(new_exp, axis=-1)
    old_weights = (old_exp / total[..., None]).astype(jnp.bfloat16)
    new_weights = (new_exp / total[..., None]).astype(jnp.bfloat16)
    mixed = jnp.einsum("rkgsc,rckd->rskgd", old_weights, values, preferred_element_type=jnp.float32)
    mixed = mixed + jnp.einsum(
        "rkgst,rtkd->rskgd", new_weights, fresh_values, preferred_element_type=jnp.float32
    )
    return mixed.reshape(rows, steps, heads_count * width).astype(jnp.bfloat16)


def owned_columns(local):
    half = lax.all_to_all(local, "tensor", split_axis=1, concat_axis=0, tiled=True)
    return lax.all_gather(half, "dp", axis=0, tiled=True)


def plain(
    token_ids, lengths, embed_table, norm_gain, w_query, w_key, w_value, w_out, q_gain, k_gain, key_cache, value_cache
):
    rows, steps = token_ids.shape
    width = q_gain.shape[0]
    every_id = lax.all_gather(token_ids, "dp", axis=0, tiled=True)
    vocab_rows = embed_table.shape[0]
    local_id = every_id - lax.axis_index("dp") * vocab_rows
    inside = (local_id >= 0) & (local_id < vocab_rows)
    picked = jnp.take(embed_table, jnp.clip(local_id, 0, vocab_rows - 1), axis=0)
    partial_rows = jnp.where(inside[..., None], picked, jnp.zeros((), jnp.bfloat16))
    own_rows = lax.psum_scatter(partial_rows, "dp", scatter_dimension=0, tiled=True)
    whole = lax.all_gather(own_rows, "tensor", axis=2, tiled=True)
    gain_full = lax.all_gather(norm_gain, "tensor", axis=0, tiled=True)
    normed = rms_scale(whole.astype(jnp.float32), gain_full).astype(jnp.bfloat16)
    flat = normed.reshape(rows * steps, -1)
    wq = owned_columns(w_query)
    wk = owned_columns(w_key)
    wv = owned_columns(w_value)
    wo = owned_columns(w_out)
    query_raw = jnp.dot(flat, wq, preferred_element_type=jnp.float32)
    key_raw = jnp.dot(flat, wk, preferred_element_type=jnp.float32)
    value_raw = jnp.dot(flat, wv, preferred_element_type=jnp.float32)
    positions = lengths[:, None] + jnp.arange(steps, dtype=jnp.int32)[None, :]
    query_raw = query_raw.reshape(rows, steps, -1, width)
    key_raw = key_raw.reshape(rows, steps, -1, width)
    fresh_values = value_raw.astype(jnp.bfloat16).reshape(rows, steps, -1, width)
    query = rotate(rms_scale(query_raw, q_gain), positions).astype(jnp.bfloat16)
    fresh_keys = rotate(rms_scale(key_raw, k_gain), positions).astype(jnp.bfloat16)
    local_heads = attend(query, fresh_keys, fresh_values, key_cache, value_cache, lengths)
    all_heads = lax.all_gather(local_heads, "tensor", axis=2, tiled=True).reshape(rows * steps, -1)
    projected = jnp.dot(all_heads, wo, preferred_element_type=jnp.float32)
    output = projected + own_rows.astype(jnp.float32).reshape(rows * steps, -1)
    attended = output.astype(jnp.bfloat16).reshape(rows, steps, -1)
    return (attended, fresh_keys.reshape(rows, steps, -1), fresh_values.reshape(rows, steps, -1))


def shards(
    token_ids,
    lengths,
    embed_table,
    norm_gain,
    w_query,
    w_key,
    w_value,
    w_out,
    q_gain,
    k_gain,
    key_cache,
    value_cache,
):
    owners = lax.axis_size("dp")
    rows, steps = token_ids.shape
    width = q_gain.shape[0]
    req, slot = requests(token_ids.reshape(-1), embed_table.shape[0], owners)
    positions = lengths[:, None] + jnp.arange(steps, dtype=jnp.int32)[None, :]
    half = width // 2
    freq = THETA ** (-(np.arange(width) % half) * 2.0 / width)
    angle = positions.astype(jnp.float32)[:, :, None] * freq.astype(np.float32)
    sign = np.where(np.arange(width) < half, -1.0, 1.0).astype(np.float32)
    cosine = jnp.cos(angle).reshape(rows * steps, width)
    sine = (jnp.sin(angle) * sign).reshape(rows * steps, width)
    attended, new_keys, new_values, flag, _, _ = step(
        lengths, req, slot, jnp.broadcast_to(norm_gain[None], (EXTRA, norm_gain.shape[0])), embed_table, w_query, w_key, w_value, w_out,
        q_gain[None], k_gain[None], cosine, sine, key_cache, value_cache,
    )
    given = (
        token_ids, lengths, embed_table, norm_gain, w_query, w_key, w_value, w_out, q_gain, k_gain,
        key_cache, value_cache,
    )
    return lax.cond(
        flag[0, 0] > 0,
        lambda: plain(*given),
        lambda: (
            attended.reshape(rows, steps, -1),
            new_keys.reshape(rows, steps, -1),
            new_values.reshape(rows, steps, -1),
        ),
    )


def solution(mesh):
    in_specs = (
        P("dp", None),
        P("dp"),
        P("dp", "tensor"),
        P("tensor"),
        P(("dp", "tensor"), None),
        P(("dp", "tensor"), None),
        P(("dp", "tensor"), None),
        P(("dp", "tensor"), None),
        P(),
        P(),
        P("dp", None, "tensor"),
        P("dp", None, "tensor"),
    )
    out_specs = (P("dp", None, "tensor"), P("dp", None, "tensor"), P("dp", None, "tensor"))
    return jax.shard_map(shards, mesh=mesh, in_specs=in_specs, out_specs=out_specs, check_vma=False)
```

```python
import math

import jax
import jax.numpy as jnp
import numpy as np
from jax import lax
from jax.experimental import pallas as pl
from jax.experimental.pallas import tpu as pltpu
from jax.sharding import PartitionSpec as P

EPS = 1e-06
THETA = 1000000.0
ROWS_AT_ONCE = 8
PIECES = 4
SLOTS = 32
LANES = 128
EXTRA = 16
MESH = pl.DeviceIdType.MESH
NT = (((1,), (1,)), ((), ()))


class Place:
    def __init__(self):
        self.dp = lax.axis_index("dp")
        self.t = lax.axis_index("tensor")
        self.y, self.xh, self.c = self.dp // 4, (self.dp // 2) % 2, self.dp % 2
        self.xl, self.z = self.t // 4, self.t % 4

    def dp_id(self, dy, dxh, dc=0):
        return ((self.y + dy) % 4) * 4 + ((self.xh + dxh) % 2) * 2 + (self.c + dc) % 2

    def t_id(self, dxl, dz):
        return ((self.xl + dxl) % 2) * 4 + (self.z + dz) % 4


def remote(src, dst, sems, k, device):
    return pltpu.make_async_remote_copy(
        src_ref=src,
        dst_ref=dst,
        send_sem=sems.at[0, k],
        recv_sem=sems.at[1, k],
        device_id=device,
        device_id_type=MESH,
    )


def greet(devices):
    barrier = pltpu.get_barrier_semaphore()
    for device in devices:
        pl.semaphore_signal(barrier, inc=1, device_id=device, device_id_type=MESH)
    pl.semaphore_wait(barrier, len(devices))


class PairRing:
    COPIES = 9

    def __init__(self, own, block, first, second, ident, device, sems, landed=None):
        self.landed = landed or (lambda k, e: None)
        self.ident = ident
        pair, nxt, prv = device(0, 1), device(1, 0), device(3, 0)
        me, mate = ident(0, 0), ident(0, 1)
        self.c = [
            remote(own, block(me), sems, 0, pair),
            remote(own, block(me), sems, 1, nxt),
            remote(own, block(me), sems, 2, prv),
            remote(block(mate), block(mate), sems, 3, nxt),
            remote(block(mate), block(mate), sems, 4, prv),
            remote(first(ident(3, 0)), first(ident(3, 0)), sems, 5, nxt),
            remote(second(ident(1, 0)), second(ident(1, 0)), sems, 6, prv),
            remote(first(ident(3, 1)), first(ident(3, 1)), sems, 7, nxt),
            remote(second(ident(1, 1)), second(ident(1, 1)), sems, 8, prv),
        ]

    def s0(self):
        self.c[0].start()
        self.c[1].start()
        self.c[2].start()

    def s1(self):
        self.c[0].wait_recv()
        self.c[3].start()
        self.c[4].start()
        self.landed(0, 1)

    def s2(self):
        self.c[1].wait_recv()
        self.c[5].start()
        self.landed(3, 0)
        self.c[2].wait_recv()
        self.c[6].start()
        self.landed(1, 0)

    def s3(self):
        self.c[3].wait_recv()
        self.c[7].start()
        self.landed(3, 1)
        self.c[4].wait_recv()
        self.c[8].start()
        self.landed(1, 1)

    def s4(self):
        self.c[5].wait_recv()
        self.c[6].wait_recv()
        self.landed(2, 0)
        self.c[7].wait_recv()
        self.c[8].wait_recv()
        self.landed(2, 1)

    def end(self):
        for copy in self.c:
            copy.wait_send()


class RingPair:
    COPIES = 8

    def __init__(self, own, block, first, second, ident, device, sems, landed=None):
        self.landed = landed or (lambda k, e: None)
        pair, nxt, prv = device(0, 1), device(1, 0), device(3, 0)
        me = ident(0, 0)
        self.c = [
            remote(own, block(me), sems, 0, nxt),
            remote(own, block(me), sems, 1, prv),
            remote(first(ident(3, 0)), first(ident(3, 0)), sems, 2, nxt),
            remote(second(ident(1, 0)), second(ident(1, 0)), sems, 3, prv),
            remote(own, block(me), sems, 4, pair),
            remote(block(ident(3, 0)), block(ident(3, 0)), sems, 5, pair),
            remote(block(ident(1, 0)), block(ident(1, 0)), sems, 6, pair),
            remote(block(ident(2, 0)), block(ident(2, 0)), sems, 7, pair),
        ]

    def s0(self):
        self.c[0].start()
        self.c[1].start()
        self.c[4].start()

    def s1(self):
        self.c[0].wait_recv()
        self.c[2].start()
        self.c[5].start()
        self.landed(3, 0)
        self.c[1].wait_recv()
        self.c[3].start()
        self.c[6].start()
        self.landed(1, 0)

    def s2(self):
        self.c[2].wait_recv()
        self.c[3].wait_recv()
        self.c[7].start()
        self.landed(2, 0)

    def s3(self):
        self.c[4].wait_recv()
        self.landed(0, 1)
        self.c[5].wait_recv()
        self.landed(3, 1)
        self.c[6].wait_recv()
        self.landed(1, 1)

    def s4(self):
        self.c[7].wait_recv()
        self.landed(2, 1)

    def end(self):
        for copy in self.c:
            copy.wait_send()


class CoreShare:
    COPIES = 8

    def __init__(self, block, place, sems):
        self.block, self.place, self.sems = block, place, sems
        self.copies = {}

    def give(self, src, k, e):
        p = self.place
        copy = remote(
            src, self.block(p.dp_id(k, e)), self.sems, k * 2 + e, (p.dp_id(0, 0, 1), p.t)
        )
        copy.start()
        self.copies[k, e] = copy

    def took(self, k, e):
        self.copies[k, e].wait_recv()

    def end(self):
        for copy in self.copies.values():
            copy.wait_send()


class Columns:
    def __init__(self, own, blocks, count, place, ring_sems, share_sems):
        cut = count * 3 // 4
        rest = count - cut

        def made(kind, start, size, sems, share_sems):
            half = size // 2
            block = lambda i: blocks(i, start, size)
            share = CoreShare(block, place, share_sems)
            ring = kind(
                own(start, size),
                block,
                lambda i: blocks(i, start, half),
                lambda i: blocks(i, start + half, size - half),
                place.dp_id,
                lambda k, e: (place.dp_id(k, e), place.t),
                sems,
                lambda k, e: share.give(block(place.dp_id(k, e)), k, e),
            )
            return ring, share

        self.a, self.share_a = made(PairRing, 0, cut, ring_sems.at[0], share_sems.at[0])
        self.b, self.share_b = made(RingPair, cut, rest, ring_sems.at[1], share_sems.at[1])
        self.mine_a, self.mine_b = own(0, cut), own(cut, rest)

    def s0(self):
        self.a.s0()
        self.b.s0()
        self.share_a.give(self.mine_a, 0, 0)
        self.share_b.give(self.mine_b, 0, 0)

    def took(self, k, e):
        self.share_a.took(k, e)
        self.share_b.took(k, e)

    def end(self):
        self.a.end()
        self.b.end()
        self.share_a.end()
        self.share_b.end()


AROUND = ((0, 0), (0, 1), (1, 0), (3, 0), (1, 1), (3, 1), (2, 0), (2, 1))


def step_kernel(
    lengths, req, slot, gain, table, wq, wk, wv, wo, q_gain, k_gain, cosine, sine, key_cache, value_cache,
    attended, new_keys, new_values, flag, wa_all, wb_all,
    reqs, slot_v, gain_v, cos_v, sin_v, index_v, slots_out, slots_in, e_own, e_v, n_v, square_v,
    wa_v, wb_v, wo_part, wo_v, heads_v, acc_a, acc_b, nk_v, nv_v, k_v, v_v, total_v,
    req_sems, slot_sems, p1_sems, o1_sems, ring_sems, share_sems,
    e_sems, heads_sems, load_sems, kv_sems, local_sems,
):
    p = Place()
    dp, t = p.dp, p.t
    owners, tensors = reqs.shape[0], e_v.shape[0]
    tokens, features = attended.shape[0], e_v.shape[2]
    vocab = table.shape[0]
    height = wq.shape[0]
    width = LANES
    rows, cache = key_cache.shape[0], key_cache.shape[1]
    steps = tokens // rows
    qw, kw = wq.shape[1] // tensors, wk.shape[1] // tensors
    ow = wo.shape[1] // tensors
    heads = qw // width
    dp_peers = [(lax.rem(dp + j, owners), t) for j in range(1, owners)]
    t_peers = [(dp, lax.rem(t + j, tensors)) for j in range(1, tensors)]
    greet(dp_peers + t_peers)

    asks = []
    for j in range(1, owners):
        to = lax.rem(dp + j, owners)
        copy = remote(req.at[to], reqs.at[dp], req_sems, j, (to, t))
        copy.start()
        asks.append(copy)
    own_ask = pltpu.make_async_copy(req.at[dp], reqs.at[dp], local_sems.at[0])
    own_ask.start()

    stored = pl.ds(pl.multiple_of((dp * tensors + t) * height, 8), height)
    hw = qw // 2
    parts = (
        (wq, qw, 0, hw, wa_all, 0),
        (wk, kw, 0, kw, wa_all, hw),
        (wv, kw, 0, kw, wa_all, hw + kw),
        (wq, qw, hw, hw, wb_all, 0),
    )

    def columns_of(w, whole, at, n, to):
        return w.at[:, pl.ds(pl.multiple_of(to * whole + at, LANES), n)]

    first = ([], [])
    for half, some in enumerate((parts[:3], parts[3:])):
        for j in range(1, tensors):
            to = lax.rem(t + j, tensors)
            for a, (w, whole, at, n, into, column) in enumerate(some):
                copy = remote(
                    columns_of(w, whole, at, n, to),
                    into.at[stored, pl.ds(column, n)],
                    p1_sems, j * 4 + half * 3 + a, (dp, to),
                )
                copy.start()
                first[half].append(copy)
        if half == 0:
            load_table = pltpu.make_async_copy(
                table, wa_v.at[pl.ds(0, vocab), pl.ds(0, features)], local_sems.at[1]
            )
            load_table.start()
    stays = [
        pltpu.make_async_copy(
            columns_of(w, whole, at, n, t), into.at[stored, pl.ds(column, n)], local_sems.at[13 + a]
        )
        for a, (w, whole, at, n, into, column) in enumerate(parts)
    ]
    stays.append(
        pltpu.make_async_copy(
            wo.at[:, pl.ds(pl.multiple_of(t * ow, LANES), ow)], wo_part.at[t], local_sems.at[5]
        )
    )
    small = [
        pltpu.make_async_copy(a, b, local_sems.at[6 + i])
        for i, (a, b) in enumerate(((slot, slot_v), (gain, gain_v), (cosine, cos_v), (sine, sin_v)))
    ]
    for copy in stays + small:
        copy.start()

    padded = -(-vocab // LANES) * LANES
    wa_v[pl.ds(vocab, padded - vocab), pl.ds(0, features)] = jnp.zeros(
        (padded - vocab, features), wa_v.dtype
    )
    for copy in asks:
        copy.wait_recv()
    own_ask.wait()
    asked = jnp.concatenate(
        [reqs[lax.rem(dp + j, owners), 0:1, :] for j in range(owners)], axis=0
    )
    over = jnp.max(jnp.where(lax.broadcasted_iota(jnp.int32, asked.shape, 1) == SLOTS, asked, 0))
    flag[0, 0] = over
    columns = jnp.transpose(asked)
    for j in range(owners):
        index_v[j * SLOTS:(j + 1) * SLOTS, :] = jnp.broadcast_to(
            columns[:SLOTS, j:j + 1], (SLOTS, LANES)
        )
    load_table.wait()

    def columns(own, block, n):
        return Columns(own, block, tensors, p, ring_sems.at[n], share_sems.at[n])

    def in_projection(ref, n):
        def block(i, at, size):
            start = pl.multiple_of((i * tensors + at) * height, 8)
            return ref.at[pl.ds(start, size * height)]

        return columns(lambda at, size: block(dp, at, size), block, n)

    cols_a = in_projection(wa_all, 0)
    cols_b = in_projection(wb_all, 1)
    outs = columns(
        lambda at, size: wo_part.at[pl.ds(at, size)],
        lambda i, at, size: wo_v.at[pl.ds(i * tensors + at, size)],
        2,
    )

    chunk = 8
    replies = []
    for m in range(owners // chunk):
        wanted = index_v[m * chunk * SLOTS:(m + 1) * chunk * SLOTS, 0:1]
        place = lax.broadcasted_iota(jnp.int32, (chunk * SLOTS, padded), 1)
        hit = (place == wanted).astype(jnp.float32).astype(jnp.bfloat16)
        picked = jnp.dot(
            hit, wa_v[0:padded, 0:features], preferred_element_type=jnp.float32
        )
        slots_out[m * chunk:(m + 1) * chunk] = picked.astype(jnp.bfloat16).reshape(
            chunk, SLOTS, features
        )
        for j in range(m * chunk, (m + 1) * chunk):
            if j == 0:
                copy = pltpu.make_async_copy(slots_out.at[0], slots_in.at[dp], local_sems.at[10])
            else:
                copy = remote(
                    slots_out.at[j], slots_in.at[dp], slot_sems, j, (lax.rem(dp + j, owners), t)
                )
            copy.start()
            replies.append(copy)

    for copy in first[0]:
        copy.wait_recv()
    for copy in stays:
        copy.wait()
    cols_a.s0()
    second = []
    for j in range(1, tensors):
        to = lax.rem(t + j, tensors)
        copy = remote(
            wo.at[:, pl.ds(pl.multiple_of(to * ow, LANES), ow)],
            wo_part.at[t],
            o1_sems, j, (dp, to),
        )
        copy.start()
        second.append(copy)

    piece = rows // PIECES

    def load_kv(n):
        i = n % PIECES
        at = pl.ds(i * piece, piece)
        return (
            pltpu.make_async_copy(key_cache.at[at], k_v.at[i % 2], kv_sems.at[0, n]),
            pltpu.make_async_copy(value_cache.at[at], v_v.at[i % 2], kv_sems.at[1, n]),
        )

    caches = [load_kv(n) for n in range(2 * PIECES)]
    for copy in caches[0] + caches[1]:
        copy.start()

    for copy in small:
        copy.wait()
    replies[0].wait()
    for copy in replies[1:]:
        copy.wait_recv()
    slots_of = jnp.transpose(slot_v[...])[:, 0:1]
    picks = lax.broadcasted_iota(jnp.int32, (tokens, owners * SLOTS), 1) == slots_of
    e_own[0:tokens] = jnp.dot(
        picks.astype(jnp.float32).astype(jnp.bfloat16),
        slots_in[...].reshape(owners * SLOTS, features),
        preferred_element_type=jnp.float32,
    ).astype(jnp.bfloat16)
    e_own[tokens:] = gain_v[...]
    e_ring = PairRing(
        e_own,
        lambda i: e_v.at[i],
        lambda i: e_v.at[i, pl.ds(0, tokens // 2)],
        lambda i: e_v.at[i, pl.ds(tokens // 2, tokens // 2 + EXTRA)],
        lambda k, e: p.t_id(e, k),
        lambda k, e: (dp, p.t_id(e, k)),
        e_sems,
    )
    e_ring.s0()
    keep_e = pltpu.make_async_copy(e_own, e_v.at[t], local_sems.at[11])
    keep_e.start()

    def square(ref):
        wide = ref[...].astype(jnp.float32)
        wide = wide * wide
        part = wide[:, 0:LANES]
        for i in range(1, features // LANES):
            part = part + wide[:, i * LANES:(i + 1) * LANES]
        return part

    def add_square(k, e):
        square_v[...] = square_v[...] + square(e_v.at[p.t_id(e, k), pl.ds(0, tokens)])

    cols_a.a.s1()
    cols_a.b.s1()
    square_v[...] = square(e_own.at[pl.ds(0, tokens)])
    e_ring.s1()
    add_square(0, 1)
    cols_a.a.s2()
    cols_a.b.s2()
    e_ring.s2()
    add_square(3, 0)
    add_square(1, 0)
    cols_a.a.s3()
    for copy in first[1]:
        copy.wait_recv()
    cols_b.s0()
    e_ring.s3()
    add_square(3, 1)
    add_square(1, 1)

    part = tensors * height
    loads = {}

    def load_all(cols, ref, into, n, places):
        for k, e in places:
            for dc in (0, 1):
                if dc:
                    cols.took(k, e)
                at = pl.multiple_of(p.dp_id(k, e, dc) * part, part)
                loads[n, k, e, dc] = pltpu.make_async_copy(
                    ref.at[pl.ds(at, part)],
                    into.at[pl.ds(at, part)],
                    load_sems.at[n, dc, k * 2 + e],
                )
                loads[n, k, e, dc].start()

    def loaded(n, places):
        for k, e in places:
            loads[n, k, e, 0].wait()
            loads[n, k, e, 1].wait()

    cols_a.b.s3()
    load_all(cols_a, wa_all, wa_v, 0, AROUND[:6])
    e_ring.s4()
    keep_e.wait()
    add_square(2, 0)
    add_square(2, 1)

    total = jnp.sum(square_v[...], axis=-1, keepdims=True)
    inverse = lax.rsqrt(total / (tensors * features) + EPS)

    def norm(i, carry):
        weight = e_v[i, pl.ds(tokens, EXTRA)].astype(jnp.float32)[0:1]
        normed = e_v[i, pl.ds(0, tokens)].astype(jnp.float32) * inverse * weight
        n_v[i] = normed.astype(jnp.bfloat16)
        return carry

    lax.fori_loop(0, tensors, norm, 0)

    def project(into, w, k, e):
        i = lax.div(p.dp_id(k, e), 2)
        into[...] = into[...] + jnp.dot(
            n_v[i],
            w[pl.ds(pl.multiple_of(i * 2 * part, 2 * part), 2 * part), :],
            preferred_element_type=jnp.float32,
        )

    def project_all(cols, ref, w, into, n):
        def early(j, carry):
            k = lax.div(j, 2)
            project(into, w, jnp.where(k == 2, 3, k), lax.rem(j, 2))
            return carry

        def late(j, carry):
            project(into, w, 2, j)
            return carry

        into[...] = jnp.zeros(into.shape, jnp.float32)
        loaded(n, AROUND[:6])
        lax.fori_loop(0, 6, early, 0)
        cols.a.s4()
        cols.b.s4()
        load_all(cols, ref, w, n, AROUND[6:])
        loaded(n, AROUND[6:])
        lax.fori_loop(0, 2, late, 0)

    cols_b.a.s1()
    cols_b.b.s1()
    project_all(cols_a, wa_all, wa_v, acc_a, 0)
    cols_b.a.s2()
    cols_b.b.s2()

    def placed(raw, head_gain):
        mean_sq = jnp.mean(raw * raw, axis=-1, keepdims=True)
        scaled = raw * lax.rsqrt(mean_sq + EPS) * head_gain
        return scaled * cos_v[...] + pltpu.roll(scaled, width // 2, 1) * sin_v[...]

    head_gain = q_gain[...].astype(jnp.float32)

    def place_heads(acc):
        for h in range(heads // 2):
            at = slice(h * width, (h + 1) * width)
            acc[:, at] = placed(acc[:, at], head_gain)

    place_heads(acc_a)
    nk_v[...] = placed(acc_a[:, hw:hw + kw], k_gain[...].astype(jnp.float32)).astype(jnp.bfloat16)
    nv_v[...] = acc_a[:, hw + kw:hw + 2 * kw].astype(jnp.bfloat16)
    new_keys[...] = nk_v[...]
    new_values[...] = nv_v[...]

    scale = 1.0 / math.sqrt(width)
    pair = 2 * steps
    group = ROWS_AT_ONCE * steps
    some = heads // 2
    count = ROWS_AT_ONCE // 2
    each = some * pair
    index = lax.broadcasted_iota(jnp.int32, (count * each, 1), 0)
    token = index // each * pair + index % pair
    is_first = lax.broadcasted_iota(jnp.int32, (each, 1), 0) % pair < steps
    fresh = lax.broadcasted_iota(jnp.int32, (count * each, group), 1)
    seen = (fresh // steps == token // steps) & (fresh <= token)
    column = lax.broadcasted_iota(jnp.int32, (count * each, cache), 1)
    none = jnp.zeros((each, width), jnp.bfloat16)

    def attend(acc, half, i, g):
        at = pl.ds(pl.multiple_of(i * piece * steps + g * group, group), group)
        queries = acc[at, 0:hw]
        keys, values = nk_v[at, :], nv_v[at, :]
        parts, scores, held = [], [], []
        for n in range(count):
            q = jnp.concatenate(
                [
                    queries[n * pair:(n + 1) * pair, h * width:(h + 1) * width]
                    for h in range(some)
                ],
                axis=0,
            ).astype(jnp.bfloat16)
            parts.append(q)
            r = g * ROWS_AT_ONCE + 2 * n
            wide_q = jnp.concatenate(
                [jnp.where(is_first, q, none), jnp.where(is_first, none, q)], axis=1
            )
            both_k = jnp.concatenate([k_v[i % 2, r], k_v[i % 2, r + 1]], axis=1)
            scores.append(
                lax.dot_general(wide_q, both_k, NT, preferred_element_type=jnp.float32)
            )
            held.append(
                jnp.where(is_first, lengths[i * piece + r], lengths[i * piece + r + 1])
            )
        new = lax.dot_general(
            jnp.concatenate(parts, axis=0), keys, NT, preferred_element_type=jnp.float32
        )
        new = jnp.where(seen, new * scale, -jnp.inf)
        old = jnp.concatenate(scores, axis=0) * scale
        old = jnp.where(column < jnp.concatenate(held, axis=0), old, -jnp.inf)
        top = jnp.maximum(
            jnp.max(old, axis=-1, keepdims=True), jnp.max(new, axis=-1, keepdims=True)
        )
        old = jnp.exp(old - top)
        new = jnp.exp(new - top)
        whole = jnp.sum(old, axis=-1, keepdims=True) + jnp.sum(new, axis=-1, keepdims=True)
        inv = 1.0 / whole
        old = (old * inv).astype(jnp.bfloat16)
        new = (new * inv).astype(jnp.bfloat16)
        out_new = jnp.dot(new, values, preferred_element_type=jnp.float32)
        results = []
        for n in range(count):
            r = g * ROWS_AT_ONCE + 2 * n
            both_v = jnp.concatenate([v_v[i % 2, r], v_v[i % 2, r + 1]], axis=1)
            mine = slice(n * each, (n + 1) * each)
            both = jnp.dot(old[mine], both_v, preferred_element_type=jnp.float32)
            out = jnp.where(is_first, both[:, :width], both[:, width:]) + out_new[mine]
            results.append(
                jnp.concatenate([out[h * pair:(h + 1) * pair] for h in range(some)], axis=1)
            )
        heads_v[half, t, at, :] = jnp.concatenate(results, axis=0).astype(jnp.bfloat16)

    span = tokens // 2

    def heads_ring(kind, half, at, n, sems):
        return kind(
            heads_v.at[half, t, pl.ds(at, n)],
            lambda i: heads_v.at[half, i, pl.ds(at, n)],
            lambda i: heads_v.at[half, i, pl.ds(at, n // 2)],
            lambda i: heads_v.at[half, i, pl.ds(at + n // 2, n // 2)],
            lambda k, e: p.t_id(e, k),
            lambda k, e: (dp, p.t_id(e, k)),
            sems,
        )

    rings = [
        heads_ring(PairRing, 0, 0, tokens, heads_sems.at[0]),
        heads_ring(PairRing, 1, 0, span, heads_sems.at[1]),
        heads_ring(RingPair, 1, span, span, heads_sems.at[2]),
    ]

    def attend_piece(acc, half, i):
        n = half * PIECES + i
        for copy in caches[n]:
            copy.wait()

        def one(g, carry):
            attend(acc, half, i, g)
            return carry

        lax.fori_loop(0, piece // ROWS_AT_ONCE, one, 0)
        if n + 2 < 2 * PIECES:
            for copy in caches[n + 2]:
                copy.start()

    attend_piece(acc_a, 0, 0)
    cols_b.a.s3()
    attend_piece(acc_a, 0, 1)
    cols_b.b.s3()
    for copy in second:
        copy.wait_recv()
    outs.s0()
    keep_o = pltpu.make_async_copy(wo_part, wo_v.at[pl.ds(dp * tensors, tensors)], local_sems.at[12])
    keep_o.start()
    load_all(cols_b, wb_all, wb_v, 1, AROUND[:6])
    attend_piece(acc_a, 0, 2)
    attend_piece(acc_a, 0, 3)
    rings[0].s0()
    project_all(cols_b, wb_all, wb_v, acc_b, 1)
    outs.a.s1()
    rings[0].s1()
    place_heads(acc_b)
    outs.b.s1()
    attend_piece(acc_b, 1, 0)
    rings[0].s2()
    outs.a.s2()
    attend_piece(acc_b, 1, 1)
    rings[1].s0()
    outs.b.s2()
    rings[0].s3()
    attend_piece(acc_b, 1, 2)
    outs.a.s3()
    rings[1].s1()
    attend_piece(acc_b, 1, 3)
    rings[2].s0()
    rings[1].s2()
    rings[2].s1()
    outs.b.s3()
    rings[1].s3()
    rings[2].s2()
    rings[0].s4()
    outs.a.s4()
    outs.b.s4()
    for k, e in AROUND:
        outs.took(k, e)
    keep_o.wait()

    per = wo_v.shape[0] // tensors // 2
    total_v[...] = e_own[pl.ds(0, tokens)].astype(jnp.float32)

    def back(half):
        def add(i, carry):
            w = wo_v[pl.ds((2 * i + half) * per, per)].reshape(hw, ow)
            total_v[...] = total_v[...] + jnp.dot(
                heads_v[half, i], w, preferred_element_type=jnp.float32
            )
            return carry

        lax.fori_loop(0, tensors, add, 0)

    back(0)
    rings[1].s4()
    rings[2].s3()
    rings[2].s4()
    back(1)
    attended[...] = total_v[...].astype(jnp.bfloat16)
    for copy in first[0] + first[1] + asks + replies[1:] + second:
        copy.wait_send()
    cols_a.end()
    cols_b.end()
    outs.end()
    e_ring.end()
    for ring in rings:
        ring.end()


def step(lengths, req, slot, gain, table, wq, wk, wv, wo, q_gain, k_gain, cosine, sine, keys, values):
    owners, tensors = lax.axis_size("dp"), lax.axis_size("tensor")
    tokens, features = slot.shape[1], table.shape[1]
    rows, cache, width = keys.shape
    height, depth = wq.shape[0], wo.shape[0]
    qw, ow = wq.shape[1] // tensors, wo.shape[1] // tensors
    hw = qw // 2
    piece = rows // PIECES
    anywhere, vmem = pl.BlockSpec(memory_space=pl.ANY), pl.BlockSpec(memory_space=pltpu.VMEM)
    smem = pl.BlockSpec(memory_space=pltpu.SMEM)
    dma = pltpu.SemaphoreType.DMA
    bf16, f32 = jnp.bfloat16, jnp.float32
    return pl.pallas_call(
        step_kernel,
        out_shape=(
            jax.ShapeDtypeStruct((tokens, ow), bf16),
            jax.ShapeDtypeStruct((tokens, width), bf16),
            jax.ShapeDtypeStruct((tokens, width), bf16),
            jax.ShapeDtypeStruct((1, 1), jnp.int32),
            jax.ShapeDtypeStruct((owners * tensors * height, hw + 2 * width), bf16),
            jax.ShapeDtypeStruct((owners * tensors * height, hw), bf16),
        ),
        in_specs=[smem] + [anywhere] * 8 + [vmem] * 2 + [anywhere] * 4,
        out_specs=(vmem, vmem, vmem, smem, anywhere, anywhere),
        scratch_shapes=[
            pltpu.VMEM((owners, 8, LANES), jnp.int32),
            pltpu.VMEM(slot.shape, jnp.int32),
            pltpu.VMEM(gain.shape, bf16),
            pltpu.VMEM(cosine.shape, f32),
            pltpu.VMEM(sine.shape, f32),
            pltpu.VMEM((owners * SLOTS, LANES), jnp.int32),
            pltpu.VMEM((owners, SLOTS, features), bf16),
            pltpu.VMEM((owners, SLOTS, features), bf16),
            pltpu.VMEM((tokens + EXTRA, features), bf16),
            pltpu.VMEM((tensors, tokens + EXTRA, features), bf16),
            pltpu.VMEM((tensors, tokens, features), bf16),
            pltpu.VMEM((tokens, LANES), f32),
            pltpu.VMEM((tensors * features, hw + 2 * width), bf16),
            pltpu.VMEM((tensors * features, hw), bf16),
            pltpu.VMEM((tensors, depth, ow), bf16),
            pltpu.VMEM((owners * tensors, depth, ow), bf16),
            pltpu.VMEM((2, tensors, tokens, hw), bf16),
            pltpu.VMEM((tokens, hw + 2 * width), f32),
            pltpu.VMEM((tokens, hw), f32),
            pltpu.VMEM((tokens, width), bf16),
            pltpu.VMEM((tokens, width), bf16),
            pltpu.VMEM((2, piece, cache, width), bf16),
            pltpu.VMEM((2, piece, cache, width), bf16),
            pltpu.VMEM((tokens, ow), f32),
            dma((2, owners)),
            dma((2, owners)),
            dma((2, 4 * tensors)),
            dma((2, tensors)),
            dma((3, 2, 2, PairRing.COPIES)),
            dma((3, 2, 2, CoreShare.COPIES)),
            dma((2, PairRing.COPIES)),
            dma((3, 2, PairRing.COPIES)),
            dma((2, 2, 8)),
            dma((2, 2 * PIECES)),
            dma((17,)),
        ],
        compiler_params=pltpu.CompilerParams(
            collective_id=1, has_side_effects=True, vmem_limit_bytes=60 * 1024 * 1024
        ),
        name="step",
    )(lengths, req, slot, gain, table, wq, wk, wv, wo, q_gain, k_gain, cosine, sine, keys, values)


def requests(ids, vocab_rows, owners):
    count = ids.shape[0]
    owner = lax.div(ids, jnp.int32(vocab_rows))
    same = ids[:, None] == ids[None, :]
    before = jnp.arange(count)[None, :] < jnp.arange(count)[:, None]
    fresh = ~jnp.any(same & before, axis=1)
    smaller = (owner[:, None] == owner[None, :]) & (ids[None, :] < ids[:, None])
    rank = jnp.sum(smaller & fresh[None, :], axis=1, dtype=jnp.int32)
    over = jnp.any(rank >= SLOTS).astype(jnp.int32)
    mine = (owner[None, None, :] == jnp.arange(owners)[:, None, None]) & (
        rank[None, None, :] == jnp.arange(SLOTS)[None, :, None]
    )
    wanted = jnp.max(jnp.where(mine, (ids - owner * vocab_rows)[None, None, :], -1), axis=-1)
    rest = jnp.full((owners, LANES - SLOTS), over, jnp.int32)
    asked = jnp.concatenate([wanted, rest], axis=1)
    req = jnp.broadcast_to(asked[:, None, :], (owners, 8, LANES))
    return req, jnp.broadcast_to((owner * SLOTS + rank)[None, :], (8, count))


def rms_scale(values, gain):
    mean_sq = jnp.mean(values * values, axis=-1, keepdims=True)
    return values * lax.rsqrt(mean_sq + EPS) * gain.astype(jnp.float32)


def rotate(values, positions):
    half = values.shape[-1] // 2
    freq = THETA ** (-jnp.arange(half, dtype=jnp.float32) * 2.0 / values.shape[-1])
    angle = positions.astype(jnp.float32)[:, :, None, None] * freq
    cosine = jnp.cos(angle)
    sine = jnp.sin(angle)
    first = values[..., :half]
    second = values[..., half:]
    return jnp.concatenate(
        [first * cosine - second * sine, second * cosine + first * sine], axis=-1
    )


def attend(query, fresh_keys, fresh_values, key_cache, value_cache, lengths):
    rows, steps, heads_count, width = query.shape
    kv_heads = fresh_keys.shape[2]
    group = heads_count // kv_heads
    cache_len = key_cache.shape[1]
    grouped = query.reshape(rows, steps, kv_heads, group, width)
    keys = key_cache.reshape(rows, cache_len, kv_heads, width)
    values = value_cache.reshape(rows, cache_len, kv_heads, width)
    scale = 1.0 / math.sqrt(width)
    old_scores = (
        jnp.einsum("rskgd,rckd->rkgsc", grouped, keys, preferred_element_type=jnp.float32) * scale
    )
    new_scores = (
        jnp.einsum("rskgd,rtkd->rkgst", grouped, fresh_keys, preferred_element_type=jnp.float32)
        * scale
    )
    valid = jnp.arange(cache_len)[None, :] < lengths[:, None]
    old_scores = jnp.where(valid[:, None, None, None, :], old_scores, -jnp.inf)
    causal = jnp.arange(steps)[None, :] <= jnp.arange(steps)[:, None]
    new_scores = jnp.where(causal[None, None, None, :, :], new_scores, -jnp.inf)
    highest = jnp.maximum(jnp.max(old_scores, axis=-1), jnp.max(new_scores, axis=-1))
    old_exp = jnp.exp(old_scores - highest[..., None])
    new_exp = jnp.exp(new_scores - highest[..., None])
    total = jnp.sum(old_exp, axis=-1) + jnp.sum(new_exp, axis=-1)
    old_weights = (old_exp / total[..., None]).astype(jnp.bfloat16)
    new_weights = (new_exp / total[..., None]).astype(jnp.bfloat16)
    mixed = jnp.einsum("rkgsc,rckd->rskgd", old_weights, values, preferred_element_type=jnp.float32)
    mixed = mixed + jnp.einsum(
        "rkgst,rtkd->rskgd", new_weights, fresh_values, preferred_element_type=jnp.float32
    )
    return mixed.reshape(rows, steps, heads_count * width).astype(jnp.bfloat16)


def owned_columns(local):
    half = lax.all_to_all(local, "tensor", split_axis=1, concat_axis=0, tiled=True)
    return lax.all_gather(half, "dp", axis=0, tiled=True)


def plain(
    token_ids, lengths, embed_table, norm_gain, w_query, w_key, w_value, w_out, q_gain, k_gain, key_cache, value_cache
):
    rows, steps = token_ids.shape
    width = q_gain.shape[0]
    every_id = lax.all_gather(token_ids, "dp", axis=0, tiled=True)
    vocab_rows = embed_table.shape[0]
    local_id = every_id - lax.axis_index("dp") * vocab_rows
    inside = (local_id >= 0) & (local_id < vocab_rows)
    picked = jnp.take(embed_table, jnp.clip(local_id, 0, vocab_rows - 1), axis=0)
    partial_rows = jnp.where(inside[..., None], picked, jnp.zeros((), jnp.bfloat16))
    own_rows = lax.psum_scatter(partial_rows, "dp", scatter_dimension=0, tiled=True)
    whole = lax.all_gather(own_rows, "tensor", axis=2, tiled=True)
    gain_full = lax.all_gather(norm_gain, "tensor", axis=0, tiled=True)
    normed = rms_scale(whole.astype(jnp.float32), gain_full).astype(jnp.bfloat16)
    flat = normed.reshape(rows * steps, -1)
    wq = owned_columns(w_query)
    wk = owned_columns(w_key)
    wv = owned_columns(w_value)
    wo = owned_columns(w_out)
    query_raw = jnp.dot(flat, wq, preferred_element_type=jnp.float32)
    key_raw = jnp.dot(flat, wk, preferred_element_type=jnp.float32)
    value_raw = jnp.dot(flat, wv, preferred_element_type=jnp.float32)
    positions = lengths[:, None] + jnp.arange(steps, dtype=jnp.int32)[None, :]
    query_raw = query_raw.reshape(rows, steps, -1, width)
    key_raw = key_raw.reshape(rows, steps, -1, width)
    fresh_values = value_raw.astype(jnp.bfloat16).reshape(rows, steps, -1, width)
    query = rotate(rms_scale(query_raw, q_gain), positions).astype(jnp.bfloat16)
    fresh_keys = rotate(rms_scale(key_raw, k_gain), positions).astype(jnp.bfloat16)
    local_heads = attend(query, fresh_keys, fresh_values, key_cache, value_cache, lengths)
    all_heads = lax.all_gather(local_heads, "tensor", axis=2, tiled=True).reshape(rows * steps, -1)
    projected = jnp.dot(all_heads, wo, preferred_element_type=jnp.float32)
    output = projected + own_rows.astype(jnp.float32).reshape(rows * steps, -1)
    attended = output.astype(jnp.bfloat16).reshape(rows, steps, -1)
    return (attended, fresh_keys.reshape(rows, steps, -1), fresh_values.reshape(rows, steps, -1))


def shards(
    token_ids,
    lengths,
    embed_table,
    norm_gain,
    w_query,
    w_key,
    w_value,
    w_out,
    q_gain,
    k_gain,
    key_cache,
    value_cache,
):
    owners = lax.axis_size("dp")
    rows, steps = token_ids.shape
    width = q_gain.shape[0]
    req, slot = requests(token_ids.reshape(-1), embed_table.shape[0], owners)
    positions = lengths[:, None] + jnp.arange(steps, dtype=jnp.int32)[None, :]
    half = width // 2
    freq = THETA ** (-(np.arange(width) % half) * 2.0 / width)
    angle = positions.astype(jnp.float32)[:, :, None] * freq.astype(np.float32)
    sign = np.where(np.arange(width) < half, -1.0, 1.0).astype(np.float32)
    cosine = jnp.cos(angle).reshape(rows * steps, width)
    sine = (jnp.sin(angle) * sign).reshape(rows * steps, width)
    attended, new_keys, new_values, flag, _, _ = step(
        lengths, req, slot, jnp.broadcast_to(norm_gain[None], (EXTRA, norm_gain.shape[0])), embed_table, w_query, w_key, w_value, w_out,
        q_gain[None], k_gain[None], cosine, sine, key_cache, value_cache,
    )
    given = (
        token_ids, lengths, embed_table, norm_gain, w_query, w_key, w_value, w_out, q_gain, k_gain,
        key_cache, value_cache,
    )
    return lax.cond(
        flag[0, 0] > 0,
        lambda: plain(*given),
        lambda: (
            attended.reshape(rows, steps, -1),
            new_keys.reshape(rows, steps, -1),
            new_values.reshape(rows, steps, -1),
        ),
    )


def solution(mesh):
    in_specs = (
        P("dp", None),
        P("dp"),
        P("dp", "tensor"),
        P("tensor"),
        P(("dp", "tensor"), None),
        P(("dp", "tensor"), None),
        P(("dp", "tensor"), None),
        P(("dp", "tensor"), None),
        P(),
        P(),
        P("dp", None, "tensor"),
        P("dp", None, "tensor"),
    )
    out_specs = (P("dp", None, "tensor"), P("dp", None, "tensor"), P("dp", None, "tensor"))
    return jax.shard_map(shards, mesh=mesh, in_specs=in_specs, out_specs=out_specs, check_vma=False)
```
